128 devices in a mesh: rows: 4 (over y), cols: 32 (over x, z, core).
Axes of the slice: x: 4, y: 4, z: 4, core: 2. Of those that a mesh axis runs over, the one named last changes fastest.
Arguments:
- object_field: bfloat16 [2, 4096, 4096], P(None, 'rows', 'cols'), may hold values from -6 to 6
- probe_mode_stack: float32 [2, 4, 256, 256], replicated, may hold values from -6 to 6
- measured: bfloat16 [4, 256, 256, 256], P('rows', 'cols'), may hold values from 0.25 to 3
- corner_row: int32 [4, 256], P('rows', 'cols'), may hold values from 0 to 4095, as said below
- corner_col: int32 [4, 256], P('rows', 'cols'), may hold values from 0 to 4095, as said below
- count: int32 [4, 32], P('rows', 'cols'), may hold values from 1 to 8, as said below
Outputs:
- object_grad: float32 [2, 4096, 4096], P(None, 'rows', 'cols')
- probe_grad: float32 [2, 4, 256, 256], replicated
The draws below stay inside these ranges and needn't reach their ends.
Inputs may be any that keep to these rules, and one draw needn't show every extreme that they name: `corner_row`: the corner of slot s of tile (a, b) lies in that tile: rows a * 1024 to (a + 1) * 1024 - 1, columns b * 128 to (b + 1) * 128 - 1. `corner_col`: same tile as corner_row. `count`: some tile has all 8 slots live.
All inputs are finite; a program needn't handle non-finite values.
Results may differ from the reference program's by a relative error of at most 0.004.
Values may be sent and summed in bfloat16 or wider, within the bound.
No kernel may reach another device: no remote copies, remote signals or barrier semaphores. Data moves between devices by JAX's collectives and lax.ppermute only.
A program may use at most 64 MiB of HBM per device.

```python
import jax
import jax.numpy as jnp
from jax import lax

WINDOW_SIDE = 256
MODES = 4
TILE_R = 1024
SLOTS = 8
TILE_C = 128
NR = 4096
NC = 4096
POS_CAP = 1024
N_ROWS = 4
N_COLS = 32


def draw_corner_row(key, part):
    key = jax.random.fold_in(key, 11)
    offset = jax.random.randint(key, (N_ROWS, N_COLS * SLOTS), 0, TILE_R)
    tile_base = (jnp.arange(N_ROWS, dtype=jnp.int32) * TILE_R)[:, None]
    return (offset + tile_base).astype(jnp.int32)


def draw_corner_col(key, part):
    key = jax.random.fold_in(key, 12)
    offset = jax.random.randint(key, (N_ROWS, N_COLS * SLOTS), 0, TILE_C)
    tile_base = (jnp.arange(N_COLS * SLOTS, dtype=jnp.int32) // SLOTS * TILE_C)[None, :]
    return (offset + tile_base).astype(jnp.int32)


def draw_count(key, part):
    key = jax.random.fold_in(key, 13)
    key_one, key_two, key_three = jax.random.split(key, 3)
    first_pick = jax.random.randint(key_one, (N_ROWS * N_COLS,), 0, SLOTS)
    second_pick = jax.random.randint(key_two, (N_ROWS * N_COLS,), 0, SLOTS)
    slot_load = jnp.minimum(first_pick, second_pick) + 1
    busiest = jax.random.randint(key_three, (), 0, N_ROWS * N_COLS)
    flat_load = jnp.where(jnp.arange(N_ROWS * N_COLS) == busiest, SLOTS, slot_load)
    return flat_load.reshape((N_ROWS, N_COLS)).astype(jnp.int32)


def level_of(rng, shape, pieces, smallest, largest):
    def one(dim, parts):
        draws = jax.random.uniform(jax.random.fold_in(jax.random.fold_in(rng, 6), dim), (parts,), jnp.float32, smallest / len(pieces), largest / len(pieces))
        return jnp.repeat(jnp.exp(draws), shape[dim] // parts).reshape((-1,) + (1,) * (len(shape) - dim - 1))

    loudness = one(*pieces[0])
    for cut in pieces[1:]:
        loudness = loudness * one(*cut)
    return loudness


def gaussian(key, shape, width, limit, cuts=(), held_as=jnp.bfloat16):
    entries = width * jax.random.normal(key, shape, jnp.float32)
    if cuts:
        entries = entries * level_of(key, shape, cuts, -0.22, 0.18)
    return jnp.clip(entries, -limit, limit).astype(held_as)


def setup_inputs(seed: int = 0) -> dict:
    key_list = jax.random.split(jax.random.key(seed), 7)
    return {
        "object_field": gaussian(key_list[0], (2, NR, NC), 1.0, 6.0, ((1, 4), (2, 32))),
        "probe_mode_stack": gaussian(key_list[1], (2, MODES, WINDOW_SIDE, WINDOW_SIDE), 1.0, 6.0, (), jnp.float32),
        "measured": jnp.clip(0.25 + 2.75 * jax.random.uniform(key_list[2], (N_ROWS, N_COLS * SLOTS, WINDOW_SIDE, WINDOW_SIDE), jnp.float32) ** level_of(key_list[2], (N_ROWS, N_COLS * SLOTS, WINDOW_SIDE, WINDOW_SIDE), ((0, 4), (1, 32)), -0.2, 0.2), 0.25, 3.0).astype(jnp.bfloat16),
        "corner_row": draw_corner_row(jax.random.fold_in(key_list[6], 71), 0),
        "corner_col": draw_corner_col(jax.random.fold_in(key_list[6], 71), 0),
        "count": draw_count(jax.random.fold_in(key_list[6], 71), 0),
    }


def dft_block(win_size):
    position = jnp.arange(win_size, dtype=jnp.int32)
    phase_index = position[:, None] * position[None, :] % win_size
    angle_value = phase_index.astype(jnp.float32) * (2.0 * jnp.pi / win_size)
    norm_factor = 1.0 / jnp.sqrt(jnp.float32(win_size))
    real_part = jnp.cos(angle_value) * norm_factor
    imag_part = -jnp.sin(angle_value) * norm_factor
    upper_half = jnp.concatenate([real_part, -imag_part], axis=1)
    lower_half = jnp.concatenate([imag_part, real_part], axis=1)
    return jnp.concatenate([upper_half, lower_half], axis=0).astype(jnp.bfloat16)

def transform(stacked, left_matrix, right_matrix):
    win_size = stacked.shape[2]
    half_done = jnp.einsum('ab,mbc->mac', left_matrix.astype(jnp.float32), stacked.astype(jnp.float32)).astype(jnp.bfloat16)
    side_by = jnp.concatenate([half_done[:, :win_size, :], half_done[:, win_size:, :]], axis=2)
    return jnp.einsum('mab,bc->mac', side_by.astype(jnp.float32), right_matrix.astype(jnp.float32))

def slot_contributions(object_window, measured_amp, probe_mode_stack, fourier_matrix):
    win_size = object_window.shape[-1]
    obj_real = object_window[0].astype(jnp.float32)
    obj_imag = object_window[1].astype(jnp.float32)
    probe_real = probe_mode_stack[0]
    probe_imag = probe_mode_stack[1]
    exit_wave = jnp.concatenate([probe_real * obj_real - probe_imag * obj_imag, probe_real * obj_imag + probe_imag * obj_real], axis=1).astype(jnp.bfloat16)
    far_field = transform(exit_wave, fourier_matrix, fourier_matrix.T)
    far_real = far_field[..., :win_size]
    far_imag = far_field[..., win_size:]
    intensity = lax.optimization_barrier(jnp.sum(far_real * far_real + far_imag * far_imag, axis=0))
    factor = 1.0 - measured_amp.astype(jnp.float32) / jnp.sqrt(intensity + 1.0)
    corrected = (far_field * jnp.concatenate([factor, factor], axis=1)).astype(jnp.bfloat16)
    restacked = jnp.concatenate([corrected[..., :win_size], corrected[..., win_size:]], axis=1)
    back_field = transform(restacked, fourier_matrix.T, fourier_matrix)
    chi_real = back_field[..., :win_size]
    chi_imag = back_field[..., win_size:]
    grad_real = lax.optimization_barrier(jnp.sum(probe_real * chi_real + probe_imag * chi_imag, axis=0))
    grad_imag = lax.optimization_barrier(jnp.sum(probe_real * chi_imag - probe_imag * chi_real, axis=0))
    term_real = obj_real * chi_real + obj_imag * chi_imag
    term_imag = obj_real * chi_imag - obj_imag * chi_real
    return (jnp.stack([grad_real, grad_imag]), jnp.stack([term_real, term_imag]))

def reference(object_field, probe_mode_stack, measured, corner_row, corner_col, count):
    fourier_matrix = dft_block(WINDOW_SIDE)
    padded = jnp.pad(object_field, ((0, 0), (0, WINDOW_SIDE), (0, WINDOW_SIDE)))
    flat_row = corner_row.reshape(-1).astype(jnp.int32)
    flat_col = corner_col.reshape(-1).astype(jnp.int32)
    flattened_measurements = measured.reshape((-1, WINDOW_SIDE, WINDOW_SIDE))
    owner_count = jnp.repeat(count.reshape(-1), SLOTS)
    slot_number = jnp.tile(jnp.arange(SLOTS, dtype=jnp.int32), N_ROWS * N_COLS)
    live_slot = slot_number < owner_count

    def visit_slot(slot_position_index, carry_pair):

        def active(state_pair):
            grad_sum, totals = state_pair
            corner_at = (jnp.int32(0), flat_row[slot_position_index], flat_col[slot_position_index])
            object_window = lax.dynamic_slice(padded, corner_at, (2, WINDOW_SIDE, WINDOW_SIDE))
            gradient_piece, probe_contribution = slot_contributions(object_window, flattened_measurements[slot_position_index], probe_mode_stack, fourier_matrix)
            grad_sum = lax.dynamic_update_slice(grad_sum, lax.dynamic_slice(grad_sum, corner_at, (2, WINDOW_SIDE, WINDOW_SIDE)) + gradient_piece, corner_at)
            return (grad_sum, totals + probe_contribution)

        def passive(state_pair):
            return state_pair
        return lax.cond(live_slot[slot_position_index], active, passive, carry_pair)
    start_pair = (jnp.zeros((2, NR + WINDOW_SIDE, NC + WINDOW_SIDE), jnp.float32), jnp.zeros((2, MODES, WINDOW_SIDE, WINDOW_SIDE), jnp.float32))
    grad_sum, totals = lax.fori_loop(0, N_ROWS * N_COLS * SLOTS, visit_slot, start_pair)
    return (grad_sum[:, :NR, :NC], totals / jnp.sqrt(jnp.float32(POS_CAP)))
```

```python
import functools

import jax
import jax.numpy as jnp
import ml_dtypes
import numpy as np
from jax import lax
from jax.experimental import pallas as pl
from jax.experimental.pallas import tpu as pltpu
from jax.sharding import PartitionSpec as P

F32 = jnp.float32
BF16 = jnp.bfloat16
LANES = 128
CHUNK = 16
BLOCK = 64


def dft_tables(win):
    half = win // 2
    k = np.arange(win)[:, None]
    j = np.arange(win)[None, :]
    angle = (k * j % win).astype(np.float64) * (2.0 * np.pi / win)
    re = np.cos(angle) / np.sqrt(win)
    im = -np.sin(angle) / np.sqrt(win)
    tables = []
    for parity in range(2):
        cr = re[parity::2, :half]
        ci = im[parity::2, :half]
        tables.append(np.block([[cr, -ci], [ci, cr]]))
    forward = np.stack(tables)
    backward = np.stack([t.T for t in tables])
    order = np.concatenate([np.arange(0, win, 2), np.arange(1, win, 2)])
    permute = np.zeros((win, win))
    permute[np.arange(win), order] = 1.0
    both = np.stack([permute, permute.T])
    cast = lambda a: a.astype(ml_dtypes.bfloat16)
    return cast(forward), cast(backward), cast(both)


def slots_kernel(
    info, fwd, bwd, probe, meas, own, own_low, nxt, nxt_low, sec, sec_low,
    g_own, g_next, g_sec, acc_keep, acc_send,
    ext, mid, acc, owin, xs, hb, gb, kb,
):
    slots = meas.shape[0]
    live = info[2 * slots]
    core = info[2 * slots + 1]
    modes = probe.shape[1]
    win = probe.shape[2]
    half = win // 2
    blocks = win // BLOCK
    tile_rows = own.shape[1]
    sums = (g_own, mid, g_sec)

    for c in range(2):
        for t, (top, bottom) in enumerate(((own, own_low), (nxt, nxt_low), (sec, sec_low))):
            ext[c, t, :tile_rows, :] = top[c].astype(F32)
            ext[c, t, tile_rows:, :] = bottom[c].astype(F32)
    for ref in sums + (acc,):
        ref[...] = jnp.zeros_like(ref)

    def slot(s, _):
        row = info[s]
        col = info[slots + s]
        left_shift = lax.rem(LANES - col, LANES)
        lane = lax.broadcasted_iota(jnp.int32, (CHUNK, LANES), 1)
        keep_left = lane < LANES - col
        keep_right = lane >= col
        sides = (slice(0, LANES), slice(LANES, 2 * LANES))

        for at in range(0, win, CHUNK):
            for c in range(2):
                parts = [
                    pltpu.roll(ext[c, t, pl.ds(row + at, CHUNK), :], left_shift, 1) for t in range(3)
                ]
                for h in range(2):
                    owin[c, h, at : at + CHUNK, :] = jnp.where(keep_left, parts[h], parts[h + 1])

        for m in range(modes):
            for at in range(0, half, CHUNK):
                for h in range(2):
                    psi = []
                    for rows in (slice(at, at + CHUNK), slice(half + at, half + at + CHUNK)):
                        p_re = probe[0, m, rows, sides[h]]
                        p_im = probe[1, m, rows, sides[h]]
                        o_re = owin[0, h, rows, :]
                        o_im = owin[1, h, rows, :]
                        psi.append((p_re * o_re - p_im * o_im, p_re * o_im + p_im * o_re))
                    for c in range(2):
                        rows = slice(c * half + at, c * half + at + CHUNK)
                        xs[m, 0, rows, sides[h]] = (psi[0][c] + psi[1][c]).astype(BF16)
                        xs[m, 1, rows, sides[h]] = (psi[0][c] - psi[1][c]).astype(BF16)
            for rp in range(2):
                v = jnp.dot(fwd[rp], xs[m, rp], preferred_element_type=F32)
                v = (
                    (v[:, :half] + v[:, half:]).astype(BF16),
                    (v[:, :half] - v[:, half:]).astype(BF16),
                )
                for pc in range(2):
                    for at in range(0, half, BLOCK):
                        for c in range(2):
                            hb[pc, (rp * half + at) // BLOCK, m * BLOCK : (m + 1) * BLOCK, sides[c]] = v[pc][
                                c * half + at : c * half + at + BLOCK
                            ]

        for rb in range(blocks):
            for pc in range(2):
                field = jnp.dot(hb[pc, rb], bwd[pc], preferred_element_type=F32)
                for at in range(0, BLOCK, CHUNK):
                    part = [field[m * BLOCK + at : m * BLOCK + at + CHUNK] for m in range(modes)]
                    total = 1.0
                    for f in part:
                        total = total + (f[:, :half] * f[:, :half] + f[:, half:] * f[:, half:])
                    f_row = rb * BLOCK + at
                    factor = 1.0 - meas[s, f_row : f_row + CHUNK, sides[pc]].astype(F32) * lax.rsqrt(total)
                    rp, f_row = divmod(f_row, half)
                    for m in range(modes):
                        for c in range(2):
                            gb[m, rp, c * half + f_row : c * half + f_row + CHUNK, sides[pc]] = (
                                part[m][:, sides[c]] * factor
                            ).astype(BF16)

        for m in range(modes):
            v0 = jnp.dot(bwd[0], gb[m, 0], preferred_element_type=F32)
            v1 = jnp.dot(bwd[1], gb[m, 1], preferred_element_type=F32)
            for side, v in enumerate(((v0 + v1).astype(BF16), (v0 - v1).astype(BF16))):
                for at in range(0, half, BLOCK):
                    for pc in range(2):
                        for c in range(2):
                            kb[pc, (side * half + at) // BLOCK, m * BLOCK : (m + 1) * BLOCK, sides[c]] = v[
                                c * half + at : c * half + at + BLOCK, sides[pc]
                            ]

        for rb in range(blocks):
            w = [jnp.dot(kb[pc, rb], fwd[pc], preferred_element_type=F32) for pc in range(2)]
            for at in range(0, BLOCK, CHUNK):
                rows = slice(rb * BLOCK + at, rb * BLOCK + at + CHUNK)
                g = [[None, None], [None, None]]
                for h in range(2):
                    o_re = owin[0, h, rows, :]
                    o_im = owin[1, h, rows, :]
                    for m in range(modes):
                        w0, w1 = (v[m * BLOCK + at : m * BLOCK + at + CHUNK] for v in w)
                        chi = w0 + w1 if h == 0 else w0 - w1
                        c_re = chi[:, :half]
                        c_im = chi[:, half:]
                        p_re = probe[0, m, rows, sides[h]]
                        p_im = probe[1, m, rows, sides[h]]
                        t_re = p_re * c_re + p_im * c_im
                        t_im = p_re * c_im - p_im * c_re
                        g[0][h] = t_re if m == 0 else g[0][h] + t_re
                        g[1][h] = t_im if m == 0 else g[1][h] + t_im
                        acc[0, m, rows, sides[h]] += o_re * c_re + o_im * c_im
                        acc[1, m, rows, sides[h]] += o_re * c_im - o_im * c_re
                for c in range(2):
                    first = pltpu.roll(g[c][0], col, 1)
                    last = pltpu.roll(g[c][1], col, 1)
                    zero = jnp.zeros_like(first)
                    spread = (
                        jnp.where(keep_right, first, zero),
                        jnp.where(keep_right, last, first),
                        jnp.where(keep_right, zero, last),
                    )
                    for t in range(3):
                        sums[t][c, pl.ds(row + rows.start, CHUNK), :] += spread[t]

        return 0

    lax.fori_loop(0, live, slot, 0)

    g_next[...] = mid[...].astype(BF16)
    for m in range(modes):
        for at in range(0, win, 8):
            for h in range(2):
                to = (m * win + at) * 2 + 8 * h
                acc_keep[to : to + 8, :] = acc[core, m, at : at + 8, h * LANES : (h + 1) * LANES]
            pair = acc[1 - core, m, at : at + 8, :]
            to = (m * win + at) * 2
            acc_send[to : to + 16, :] = jnp.concatenate([pair[:, :LANES], pair[:, LANES:]], axis=0).astype(BF16)


def prepare_kernel(fwd, bwd, perm, probe, meas, fwd_out, bwd_out, probe_out, meas_out, swaps, raw, sems):
    copies = [
        pltpu.make_async_copy(source, target, sems.at[i])
        for i, (source, target) in enumerate(
            ((perm, swaps), (meas.at[0], raw), (probe, probe_out), (fwd, fwd_out), (bwd, bwd_out))
        )
    ]
    for copy in copies:
        copy.start()
    copies[0].wait()
    copies[1].wait()
    for s in range(raw.shape[0]):
        rows_done = jnp.dot(swaps[0], raw[s], preferred_element_type=F32).astype(BF16)
        meas_out[s] = jnp.dot(rows_done, swaps[1], preferred_element_type=F32).astype(BF16)
    for copy in copies[2:]:
        copy.wait()


def prepare(probe, measured):
    slots, win = measured.shape[1:3]
    fwd, bwd, perm = dft_tables(win)
    return pl.pallas_call(
        prepare_kernel,
        in_specs=[pl.BlockSpec(memory_space=pltpu.HBM)] * 5,
        out_specs=[pl.BlockSpec(memory_space=pltpu.VMEM)] * 4,
        out_shape=[
            jax.ShapeDtypeStruct(fwd.shape, BF16),
            jax.ShapeDtypeStruct(bwd.shape, BF16),
            jax.ShapeDtypeStruct(probe.shape, F32),
            jax.ShapeDtypeStruct(measured.shape[1:], BF16),
        ],
        scratch_shapes=[
            pltpu.VMEM(perm.shape, BF16),
            pltpu.VMEM(measured.shape[1:], BF16),
            pltpu.SemaphoreType.DMA((5,)),
        ],
        cost_estimate=pl.CostEstimate(flops=4 * slots * win**3, bytes_accessed=8 << 20, transcendentals=0),
        compiler_params=pltpu.CompilerParams(vmem_limit_bytes=8 * 1024 * 1024),
        name="prepare",
    )(jnp.asarray(fwd), jnp.asarray(bwd), jnp.asarray(perm), probe, measured)


def run_slots(info, fwd, bwd, probe, measured, own, own_low, nxt, nxt_low, sec, sec_low):
    tile_rows, tile_cols = own.shape[1:]
    modes, win = probe.shape[1:3]
    tall = (2, tile_rows + win, tile_cols)
    flat = (2 * modes * win, LANES)
    blocks = (2, win // BLOCK, modes * BLOCK, win)
    vmem = pl.BlockSpec(memory_space=pltpu.VMEM)
    return pl.pallas_call(
        slots_kernel,
        in_specs=[pl.BlockSpec(memory_space=pltpu.SMEM)] + [vmem] * 10,
        out_specs=[vmem] * 5,
        out_shape=[
            jax.ShapeDtypeStruct(tall, F32),
            jax.ShapeDtypeStruct(tall, BF16),
            jax.ShapeDtypeStruct(tall, F32),
            jax.ShapeDtypeStruct(flat, F32),
            jax.ShapeDtypeStruct(flat, BF16),
        ],
        scratch_shapes=[
            pltpu.VMEM((2, 3) + tall[1:], F32),
            pltpu.VMEM(tall, F32),
            pltpu.VMEM((2, modes, win, win), F32),
            pltpu.VMEM((2, 2, win, LANES), F32),
            pltpu.VMEM((modes, 2, win, win), BF16),
            pltpu.VMEM(blocks, BF16),
            pltpu.VMEM((modes, 2, win, win), BF16),
            pltpu.VMEM(blocks, BF16),
        ],
        compiler_params=pltpu.CompilerParams(vmem_limit_bytes=24 * 1024 * 1024),
        name="slots",
    )(info, fwd, bwd, probe, measured, own, own_low, nxt, nxt_low, sec, sec_low)


def moved(value, target):
    n_rows = lax.axis_size("rows")
    n_cols = lax.axis_size("cols")
    pairs = []
    for a in range(n_rows):
        for b in range(n_cols):
            to_a, to_b = target(a, b)
            if 0 <= to_a < n_rows and 0 <= to_b < n_cols:
                pairs.append((a * n_cols + b, to_a * n_cols + to_b))
    return lax.ppermute(value, ("rows", "cols"), pairs)


def swap_cores(value):
    return moved(value, lambda a, b: (a, b ^ 1))


def local(object_field, probe_mode_stack, measured, corner_row, corner_col, count):
    tile_rows, tile_cols = object_field.shape[1:]
    modes, win = probe_mode_stack.shape[1:3]
    slot_count = measured.shape[1]
    devices = lax.axis_size("rows") * lax.axis_size("cols")
    col_at = lax.axis_index("cols")
    core = lax.rem(col_at, 2)

    top = object_field[:, :win, :]
    sec = moved(object_field, lambda a, b: (a, b - 2))
    sec_low = moved(top, lambda a, b: (a - 1, b - 2))
    own_low = moved(top, lambda a, b: (a - 1, b))
    prepared, sec = lax.optimization_barrier((prepare(probe_mode_stack, measured), sec))
    nxt_low = swap_cores(jnp.where(core == 0, sec_low, own_low))
    nxt = swap_cores(jnp.where(core == 0, sec, object_field))
    info = jnp.concatenate(
        [
            corner_row[0] - lax.axis_index("rows") * tile_rows,
            corner_col[0] - col_at * tile_cols,
            count[0],
            core[None],
        ]
    )
    g_own, g_next, g_sec, acc_keep, acc_send = run_slots(
        info, *prepared, object_field, own_low, nxt, nxt_low, sec, sec_low
    )

    acc_got = swap_cores(acc_send)
    near = swap_cores(g_next)
    chip_sum = (acc_keep + acc_got.astype(F32)).astype(BF16)
    chip_sum, near = lax.optimization_barrier((chip_sum, near))
    near = near.astype(F32)
    none = jnp.zeros_like(near)
    outward = (g_sec + jnp.where(core == 0, near, none)).astype(BF16)
    far = moved(outward, lambda a, b: (a, b + 2))
    total = g_own + jnp.where(core == 1, near, none) + far.astype(F32)
    rim = moved(total[:, tile_rows:].astype(BF16), lambda a, b: (a + 1, b))

    groups = [[i for i in range(devices) if i % 2 == c] for c in range(2)]
    exchange = functools.partial(
        lax.all_to_all, axis_name=("rows", "cols"), split_axis=0, concat_axis=0,
        axis_index_groups=groups, tiled=True,
    )
    share = exchange(chip_sum.reshape(devices // 2, -1, LANES))
    scale = 1.0 / jnp.sqrt(jnp.float32(devices * slot_count))
    share = (jnp.sum(share.astype(F32), axis=0) * scale).astype(BF16)
    mine = exchange(jnp.broadcast_to(share[None], (devices // 2,) + share.shape))
    mine, rim = lax.optimization_barrier((mine, rim))
    mine = mine.reshape(-1, LANES)
    part = lax.broadcasted_iota(jnp.int32, (2,) + mine.shape, 0)
    probe_grad = jnp.where(part == core, mine[None], swap_cores(mine)[None]).astype(F32)
    probe_grad = probe_grad.reshape(2, modes, win // 8, 2, 8, LANES).transpose(0, 1, 2, 4, 3, 5)
    probe_grad = probe_grad.reshape(2, modes, win, win)

    object_grad = total[:, :tile_rows] + jnp.pad(rim.astype(F32), ((0, 0), (0, tile_rows - win), (0, 0)))
    return (object_grad, probe_grad)


def solution(mesh):
    placed = (
        P(None, "rows", "cols"),
        P(),
        P("rows", "cols", None, None),
        P("rows", "cols"),
        P("rows", "cols"),
        P("rows", "cols"),
    )
    return jax.shard_map(
        local, mesh=mesh, in_specs=placed, out_specs=(P(None, "rows", "cols"), P()), check_vma=False
    )
```

```python
import functools

import jax
import jax.numpy as jnp
import ml_dtypes
import numpy as np
from jax import lax
from jax.experimental import pallas as pl
from jax.experimental.pallas import tpu as pltpu
from jax.sharding import PartitionSpec as P

F32 = jnp.float32
BF16 = jnp.bfloat16
LANES = 128
CHUNK = 16
BLOCK = 64


def dft_tables(win):
    half = win // 2
    k = np.arange(win)[:, None]
    j = np.arange(win)[None, :]
    angle = (k * j % win).astype(np.float64) * (2.0 * np.pi / win)
    re = np.cos(angle) / np.sqrt(win)
    im = -np.sin(angle) / np.sqrt(win)
    tables = []
    for parity in range(2):
        cr = re[parity::2, :half]
        ci = im[parity::2, :half]
        tables.append(np.block([[cr, -ci], [ci, cr]]))
    forward = np.stack(tables)
    backward = np.stack([t.T for t in tables])
    order = np.concatenate([np.arange(0, win, 2), np.arange(1, win, 2)])
    permute = np.zeros((win, win))
    permute[np.arange(win), order] = 1.0
    both = np.stack([permute, permute.T])
    cast = lambda a: a.astype(ml_dtypes.bfloat16)
    return cast(forward), cast(backward), cast(both)


def slots_kernel(
    info, fwd, bwd, probe, meas, own, own_low, nxt, nxt_low, sec, sec_low,
    g_own, g_next, g_next_low, g_sec, acc_keep, acc_send,
    ext, mid, acc, owin, xs, hb, gb, kb,
):
    slots = meas.shape[0]
    live = info[2 * slots]
    core = info[2 * slots + 1]
    modes = probe.shape[1]
    win = probe.shape[2]
    half = win // 2
    blocks = win // BLOCK
    tile_rows = own.shape[1]
    sums = (g_own, mid, g_sec)

    for c in range(2):
        for t, (top, bottom) in enumerate(((own, own_low), (nxt, nxt_low), (sec, sec_low))):
            ext[c, t, :tile_rows, :] = top[c].astype(F32)
            ext[c, t, tile_rows:, :] = bottom[c].astype(F32)
    for ref in sums + (acc,):
        ref[...] = jnp.zeros_like(ref)

    sides = (slice(0, LANES), slice(LANES, 2 * LANES))
    lane = lax.broadcasted_iota(jnp.int32, (CHUNK, LANES), 1)

    def pair_of_slots(pair, _):
        whole = 2 * pair + 1 < live
        slot = (2 * pair, jnp.where(whole, 2 * pair + 1, 2 * pair))
        weight = (None, jnp.where(whole, 1.0, 0.0).astype(F32))
        row = [info[s] for s in slot]
        col = [info[slots + s] for s in slot]
        left_shift = [lax.rem(LANES - c, LANES) for c in col]
        keep_left = [lane < LANES - c for c in col]
        keep_right = [lane >= c for c in col]

        for q in range(2):
            for at in range(0, win, CHUNK):
                for c in range(2):
                    parts = [
                        pltpu.roll(ext[c, t, pl.ds(row[q] + at, CHUNK), :], left_shift[q], 1) for t in range(3)
                    ]
                    for h in range(2):
                        owin[q, c, h, at : at + CHUNK, :] = jnp.where(keep_left[q], parts[h], parts[h + 1])

        for m in range(modes):
            for at in range(0, half, CHUNK):
                for h in range(2):
                    psi = ([], [])
                    for rows in (slice(at, at + CHUNK), slice(half + at, half + at + CHUNK)):
                        p_re = probe[0, m, rows, sides[h]]
                        p_im = probe[1, m, rows, sides[h]]
                        for q in range(2):
                            o_re = owin[q, 0, h, rows, :]
                            o_im = owin[q, 1, h, rows, :]
                            psi[q].append((p_re * o_re - p_im * o_im, p_re * o_im + p_im * o_re))
                    for q in range(2):
                        for c in range(2):
                            rows = slice(c * half + at, c * half + at + CHUNK)
                            xs[q, m, 0, rows, sides[h]] = (psi[q][0][c] + psi[q][1][c]).astype(BF16)
                            xs[q, m, 1, rows, sides[h]] = (psi[q][0][c] - psi[q][1][c]).astype(BF16)
            for q in range(2):
                for rp in range(2):
                    v = jnp.dot(fwd[rp], xs[q, m, rp], preferred_element_type=F32)
                    v = (
                        (v[:, :half] + v[:, half:]).astype(BF16),
                        (v[:, :half] - v[:, half:]).astype(BF16),
                    )
                    for pc in range(2):
                        for at in range(0, half, BLOCK):
                            for c in range(2):
                                hb[
                                    q, pc, (rp * half + at) // BLOCK, m * BLOCK : (m + 1) * BLOCK, sides[c]
                                ] = v[pc][c * half + at : c * half + at + BLOCK]

        for rb in range(blocks):
            for pc in range(2):
                for q in range(2):
                    field = jnp.dot(hb[q, pc, rb], bwd[pc], preferred_element_type=F32)
                    for at in range(0, BLOCK, CHUNK):
                        part = [field[m * BLOCK + at : m * BLOCK + at + CHUNK] for m in range(modes)]
                        total = 1.0
                        for f in part:
                            total = total + (f[:, :half] * f[:, :half] + f[:, half:] * f[:, half:])
                        f_row = rb * BLOCK + at
                        factor = 1.0 - meas[slot[q], f_row : f_row + CHUNK, sides[pc]].astype(F32) * lax.rsqrt(total)
                        if q == 1:
                            factor = factor * weight[q]
                        rp, f_row = divmod(f_row, half)
                        for m in range(modes):
                            for c in range(2):
                                gb[q, m, rp, c * half + f_row : c * half + f_row + CHUNK, sides[pc]] = (
                                    part[m][:, sides[c]] * factor
                                ).astype(BF16)

        for m in range(modes):
            for q in range(2):
                v0 = jnp.dot(bwd[0], gb[q, m, 0], preferred_element_type=F32)
                v1 = jnp.dot(bwd[1], gb[q, m, 1], preferred_element_type=F32)
                for side, v in enumerate(((v0 + v1).astype(BF16), (v0 - v1).astype(BF16))):
                    for at in range(0, half, BLOCK):
                        for pc in range(2):
                            for c in range(2):
                                kb[
                                    q, pc, (side * half + at) // BLOCK, m * BLOCK : (m + 1) * BLOCK, sides[c]
                                ] = v[c * half + at : c * half + at + BLOCK, sides[pc]]

        for rb in range(blocks):
            w = [
                [jnp.dot(kb[q, pc, rb], fwd[pc], preferred_element_type=F32) for pc in range(2)]
                for q in range(2)
            ]
            for at in range(0, BLOCK, CHUNK):
                rows = slice(rb * BLOCK + at, rb * BLOCK + at + CHUNK)
                g = [[[None, None], [None, None]] for q in range(2)]
                for h in range(2):
                    o = [[owin[q, c, h, rows, :] for c in range(2)] for q in range(2)]
                    for m in range(modes):
                        p_re = probe[0, m, rows, sides[h]]
                        p_im = probe[1, m, rows, sides[h]]
                        terms = []
                        for q in range(2):
                            w0, w1 = (v[m * BLOCK + at : m * BLOCK + at + CHUNK] for v in w[q])
                            chi = w0 + w1 if h == 0 else w0 - w1
                            c_re = chi[:, :half]
                            c_im = chi[:, half:]
                            t_re = p_re * c_re + p_im * c_im
                            t_im = p_re * c_im - p_im * c_re
                            g[q][0][h] = t_re if m == 0 else g[q][0][h] + t_re
                            g[q][1][h] = t_im if m == 0 else g[q][1][h] + t_im
                            o_re, o_im = o[q]
                            terms.append((o_re * c_re + o_im * c_im, o_re * c_im - o_im * c_re))
                        for c in range(2):
                            acc[c, m, rows, sides[h]] += terms[0][c] + terms[1][c]
                for q in range(2):
                    for c in range(2):
                        left = pltpu.roll(g[q][c][0], col[q], 1)
                        right = pltpu.roll(g[q][c][1], col[q], 1)
                        zero = jnp.zeros_like(left)
                        spread = (
                            jnp.where(keep_right[q], left, zero),
                            jnp.where(keep_right[q], right, left),
                            jnp.where(keep_right[q], zero, right),
                        )
                        for t in range(3):
                            sums[t][c, pl.ds(row[q] + rows.start, CHUNK), :] += spread[t]
        return 0

    lax.fori_loop(0, lax.div(live + 1, 2), pair_of_slots, 0)

    g_next[...] = mid[:, :tile_rows, :].astype(BF16)
    g_next_low[...] = mid[:, tile_rows:, :].astype(BF16)
    for m in range(modes):
        for at in range(0, win, 8):
            for h in range(2):
                to = (m * win + at) * 2 + 8 * h
                acc_keep[to : to + 8, :] = acc[core, m, at : at + 8, h * LANES : (h + 1) * LANES]
            pair = acc[1 - core, m, at : at + 8, :]
            to = (m * win + at) * 2
            acc_send[to : to + 16, :] = jnp.concatenate([pair[:, :LANES], pair[:, LANES:]], axis=0).astype(BF16)


def prepare_kernel(fwd, bwd, perm, probe, meas, fwd_out, bwd_out, probe_out, meas_out, swaps, raw, sems):
    copies = [
        pltpu.make_async_copy(source, target, sems.at[i])
        for i, (source, target) in enumerate(
            ((perm, swaps), (meas.at[0], raw), (probe, probe_out), (fwd, fwd_out), (bwd, bwd_out))
        )
    ]
    for copy in copies:
        copy.start()
    copies[0].wait()
    copies[1].wait()
    for s in range(raw.shape[0]):
        rows_done = jnp.dot(swaps[0], raw[s], preferred_element_type=F32).astype(BF16)
        meas_out[s] = jnp.dot(rows_done, swaps[1], preferred_element_type=F32).astype(BF16)
    for copy in copies[2:]:
        copy.wait()


def prepare(probe, measured):
    slots, win = measured.shape[1:3]
    fwd, bwd, perm = dft_tables(win)
    return pl.pallas_call(
        prepare_kernel,
        in_specs=[pl.BlockSpec(memory_space=pltpu.HBM)] * 5,
        out_specs=[pl.BlockSpec(memory_space=pltpu.VMEM)] * 4,
        out_shape=[
            jax.ShapeDtypeStruct(fwd.shape, BF16),
            jax.ShapeDtypeStruct(bwd.shape, BF16),
            jax.ShapeDtypeStruct(probe.shape, F32),
            jax.ShapeDtypeStruct(measured.shape[1:], BF16),
        ],
        scratch_shapes=[
            pltpu.VMEM(perm.shape, BF16),
            pltpu.VMEM(measured.shape[1:], BF16),
            pltpu.SemaphoreType.DMA((5,)),
        ],
        cost_estimate=pl.CostEstimate(flops=4 * slots * win**3, bytes_accessed=8 << 20, transcendentals=0),
        compiler_params=pltpu.CompilerParams(vmem_limit_bytes=8 * 1024 * 1024),
        name="prepare",
    )(jnp.asarray(fwd), jnp.asarray(bwd), jnp.asarray(perm), probe, measured)


def run_slots(info, fwd, bwd, probe, measured, own, own_low, nxt, nxt_low, sec, sec_low):
    tile_rows, tile_cols = own.shape[1:]
    modes, win = probe.shape[1:3]
    tall = (2, tile_rows + win, tile_cols)
    flat = (2 * modes * win, LANES)
    blocks = (2, win // BLOCK, modes * BLOCK, win)
    vmem = pl.BlockSpec(memory_space=pltpu.VMEM)
    return pl.pallas_call(
        slots_kernel,
        in_specs=[pl.BlockSpec(memory_space=pltpu.SMEM)] + [vmem] * 10,
        out_specs=[vmem] * 6,
        out_shape=[
            jax.ShapeDtypeStruct(tall, F32),
            jax.ShapeDtypeStruct(own.shape, BF16),
            jax.ShapeDtypeStruct(own_low.shape, BF16),
            jax.ShapeDtypeStruct(tall, F32),
            jax.ShapeDtypeStruct(flat, F32),
            jax.ShapeDtypeStruct(flat, BF16),
        ],
        scratch_shapes=[
            pltpu.VMEM((2, 3) + tall[1:], F32),
            pltpu.VMEM(tall, F32),
            pltpu.VMEM((2, modes, win, win), F32),
            pltpu.VMEM((2, 2, 2, win, LANES), F32),
            pltpu.VMEM((2, modes, 2, win, win), BF16),
            pltpu.VMEM((2,) + blocks, BF16),
            pltpu.VMEM((2, modes, 2, win, win), BF16),
            pltpu.VMEM((2,) + blocks, BF16),
        ],
        compiler_params=pltpu.CompilerParams(vmem_limit_bytes=32 * 1024 * 1024),
        name="slots",
    )(info, fwd, bwd, probe, measured, own, own_low, nxt, nxt_low, sec, sec_low)


def moved(value, target):
    n_rows = lax.axis_size("rows")
    n_cols = lax.axis_size("cols")
    pairs = []
    for a in range(n_rows):
        for b in range(n_cols):
            to_a, to_b = target(a, b)
            if 0 <= to_a < n_rows and 0 <= to_b < n_cols:
                pairs.append((a * n_cols + b, to_a * n_cols + to_b))
    return lax.ppermute(value, ("rows", "cols"), pairs)


def swap_cores(value):
    return moved(value, lambda a, b: (a, b ^ 1))


def local(object_field, probe_mode_stack, measured, corner_row, corner_col, count):
    tile_rows, tile_cols = object_field.shape[1:]
    modes, win = probe_mode_stack.shape[1:3]
    slot_count = measured.shape[1]
    devices = lax.axis_size("rows") * lax.axis_size("cols")
    col_at = lax.axis_index("cols")
    core = lax.rem(col_at, 2)

    top = object_field[:, :win, :]
    sec = moved(object_field, lambda a, b: (a, b - 2))
    sec_low = moved(top, lambda a, b: (a - 1, b - 2))
    own_low = moved(top, lambda a, b: (a - 1, b))
    prepared, sec = lax.optimization_barrier((prepare(probe_mode_stack, measured), sec))
    nxt_low = swap_cores(jnp.where(core == 0, sec_low, own_low))
    nxt = swap_cores(jnp.where(core == 0, sec, object_field))
    info = jnp.concatenate(
        [
            corner_row[0] - lax.axis_index("rows") * tile_rows,
            corner_col[0] - col_at * tile_cols,
            count[0],
            core[None],
        ]
    )
    g_own, g_next, g_next_low, g_sec, acc_keep, acc_send = run_slots(
        info, *prepared, object_field, own_low, nxt, nxt_low, sec, sec_low
    )

    acc_got = swap_cores(acc_send)
    near = swap_cores(g_next)
    chip_sum = (acc_keep + acc_got.astype(F32)).astype(BF16)
    chip_sum, near, near_low = lax.optimization_barrier((chip_sum, near, g_next_low))
    near = jnp.concatenate([near, swap_cores(near_low)], axis=1).astype(F32)
    none = jnp.zeros_like(near)
    outward = (g_sec + jnp.where(core == 0, near, none)).astype(BF16)
    far = moved(outward, lambda a, b: (a, b + 2))
    total = g_own + jnp.where(core == 1, near, none) + far.astype(F32)
    rim = moved(total[:, tile_rows:].astype(BF16), lambda a, b: (a + 1, b))

    groups = [[i for i in range(devices) if i % 2 == c] for c in range(2)]
    exchange = functools.partial(
        lax.all_to_all, axis_name=("rows", "cols"), split_axis=0, concat_axis=0,
        axis_index_groups=groups, tiled=True,
    )
    share = exchange(chip_sum.reshape(devices // 2, -1, LANES))
    scale = 1.0 / jnp.sqrt(jnp.float32(devices * slot_count))
    share = (jnp.sum(share.astype(F32), axis=0) * scale).astype(BF16)
    mine = exchange(jnp.broadcast_to(share[None], (devices // 2,) + share.shape))
    mine, rim = lax.optimization_barrier((mine, rim))
    mine = mine.reshape(-1, LANES)
    part = lax.broadcasted_iota(jnp.int32, (2,) + mine.shape, 0)
    probe_grad = jnp.where(part == core, mine[None], swap_cores(mine)[None]).astype(F32)
    probe_grad = probe_grad.reshape(2, modes, win // 8, 2, 8, LANES).transpose(0, 1, 2, 4, 3, 5)
    probe_grad = probe_grad.reshape(2, modes, win, win)

    object_grad = total[:, :tile_rows] + jnp.pad(rim.astype(F32), ((0, 0), (0, tile_rows - win), (0, 0)))
    return (object_grad, probe_grad)


def solution(mesh):
    placed = (
        P(None, "rows", "cols"),
        P(),
        P("rows", "cols", None, None),
        P("rows", "cols"),
        P("rows", "cols"),
        P("rows", "cols"),
    )
    return jax.shard_map(
        local, mesh=mesh, in_specs=placed, out_specs=(P(None, "rows", "cols"), P()), check_vma=False
    )
```

```python
import functools

import jax
import jax.numpy as jnp
import ml_dtypes
import numpy as np
from jax import lax
from jax.experimental import pallas as pl
from jax.experimental.pallas import tpu as pltpu
from jax.sharding import PartitionSpec as P

F32 = jnp.float32
BF16 = jnp.bfloat16
LANES = 128
CHUNK = 16
BLOCK = 64


def dft_tables(win):
    half = win // 2
    k = np.arange(win)[:, None]
    j = np.arange(win)[None, :]
    angle = (k * j % win).astype(np.float64) * (2.0 * np.pi / win)
    re = np.cos(angle) / np.sqrt(win)
    im = -np.sin(angle) / np.sqrt(win)
    tables = []
    for parity in range(2):
        cr = re[parity::2, :half]
        ci = im[parity::2, :half]
        tables.append(np.block([[cr, -ci], [ci, cr]]))
    forward = np.stack(tables)
    backward = np.stack([t.T for t in tables])
    order = np.concatenate([np.arange(0, win, 2), np.arange(1, win, 2)])
    permute = np.zeros((win, win))
    permute[np.arange(win), order] = 1.0
    both = np.stack([permute, permute.T])
    cast = lambda a: a.astype(ml_dtypes.bfloat16)
    return cast(forward), cast(backward), cast(both)


def slots_kernel(
    info, fwd, bwd, probe, meas, own, own_low, nxt, nxt_low, sec, sec_low,
    g_own, g_next, g_sec, acc_keep, acc_send,
    ext, mid, acc, owin, xs, hb, gb, kb,
):
    slots = meas.shape[0]
    live = info[2 * slots]
    core = info[2 * slots + 1]
    modes = probe.shape[1]
    win = probe.shape[2]
    half = win // 2
    blocks = win // BLOCK
    tile_rows = own.shape[1]
    sums = (g_own, mid, g_sec)

    for c in range(2):
        for t, (top, bottom) in enumerate(((own, own_low), (nxt, nxt_low), (sec, sec_low))):
            ext[c, t, :tile_rows, :] = top[c].astype(F32)
            ext[c, t, tile_rows:, :] = bottom[c].astype(F32)
    for ref in sums + (acc,):
        ref[...] = jnp.zeros_like(ref)

    sides = (slice(0, LANES), slice(LANES, 2 * LANES))
    lane = lax.broadcasted_iota(jnp.int32, (CHUNK, LANES), 1)

    def pair_of_slots(pair, _):
        whole = 2 * pair + 1 < live
        slot = (2 * pair, jnp.where(whole, 2 * pair + 1, 2 * pair))
        weight = (None, jnp.where(whole, 1.0, 0.0).astype(F32))
        row = [info[s] for s in slot]
        col = [info[slots + s] for s in slot]
        left_shift = [lax.rem(LANES - c, LANES) for c in col]
        keep_left = [lane < LANES - c for c in col]
        keep_right = [lane >= c for c in col]

        for q in range(2):
            for at in range(0, win, CHUNK):
                for c in range(2):
                    parts = [
                        pltpu.roll(ext[c, t, pl.ds(row[q] + at, CHUNK), :], left_shift[q], 1) for t in range(3)
                    ]
                    for h in range(2):
                        owin[q, c, h, at : at + CHUNK, :] = jnp.where(keep_left[q], parts[h], parts[h + 1])

        for m in range(modes):
            for at in range(0, half, CHUNK):
                for h in range(2):
                    psi = ([], [])
                    for rows in (slice(at, at + CHUNK), slice(half + at, half + at + CHUNK)):
                        p_re = probe[0, m, rows, sides[h]]
                        p_im = probe[1, m, rows, sides[h]]
                        for q in range(2):
                            o_re = owin[q, 0, h, rows, :]
                            o_im = owin[q, 1, h, rows, :]
                            psi[q].append((p_re * o_re - p_im * o_im, p_re * o_im + p_im * o_re))
                    for q in range(2):
                        for c in range(2):
                            rows = slice(c * half + at, c * half + at + CHUNK)
                            xs[q, m, 0, rows, sides[h]] = (psi[q][0][c] + psi[q][1][c]).astype(BF16)
                            xs[q, m, 1, rows, sides[h]] = (psi[q][0][c] - psi[q][1][c]).astype(BF16)
            for q in range(2):
                for rp in range(2):
                    v = jnp.dot(fwd[rp], xs[q, m, rp], preferred_element_type=F32)
                    v = (
                        (v[:, :half] + v[:, half:]).astype(BF16),
                        (v[:, :half] - v[:, half:]).astype(BF16),
                    )
                    for pc in range(2):
                        for at in range(0, half, BLOCK):
                            for c in range(2):
                                first = (q * modes + m) * BLOCK
                                hb[pc, (rp * half + at) // BLOCK, first : first + BLOCK, sides[c]] = v[pc][c * half + at : c * half + at + BLOCK]

        for rb in range(blocks):
            for pc in range(2):
                fields = jnp.dot(hb[pc, rb], bwd[pc], preferred_element_type=F32)
                for q in range(2):
                    field = fields[q * modes * BLOCK : (q + 1) * modes * BLOCK]
                    for at in range(0, BLOCK, CHUNK):
                        part = [field[m * BLOCK + at : m * BLOCK + at + CHUNK] for m in range(modes)]
                        total = 1.0
                        for f in part:
                            total = total + (f[:, :half] * f[:, :half] + f[:, half:] * f[:, half:])
                        f_row = rb * BLOCK + at
                        factor = 1.0 - meas[slot[q], f_row : f_row + CHUNK, sides[pc]].astype(F32) * lax.rsqrt(total)
                        if q == 1:
                            factor = factor * weight[q]
                        rp, f_row = divmod(f_row, half)
                        for m in range(modes):
                            for c in range(2):
                                gb[q, m, rp, c * half + f_row : c * half + f_row + CHUNK, sides[pc]] = (
                                    part[m][:, sides[c]] * factor
                                ).astype(BF16)

        for m in range(modes):
            for q in range(2):
                v0 = jnp.dot(bwd[0], gb[q, m, 0], preferred_element_type=F32)
                v1 = jnp.dot(bwd[1], gb[q, m, 1], preferred_element_type=F32)
                for side, v in enumerate(((v0 + v1).astype(BF16), (v0 - v1).astype(BF16))):
                    for at in range(0, half, BLOCK):
                        for pc in range(2):
                            for c in range(2):
                                first = (q * modes + m) * BLOCK
                                kb[pc, (side * half + at) // BLOCK, first : first + BLOCK, sides[c]] = v[c * half + at : c * half + at + BLOCK, sides[pc]]

        for rb in range(blocks):
            fields = [jnp.dot(kb[pc, rb], fwd[pc], preferred_element_type=F32) for pc in range(2)]
            w = [[f[q * modes * BLOCK : (q + 1) * modes * BLOCK] for f in fields] for q in range(2)]
            for at in range(0, BLOCK, CHUNK):
                rows = slice(rb * BLOCK + at, rb * BLOCK + at + CHUNK)
                g = [[[None, None], [None, None]] for q in range(2)]
                for h in range(2):
                    o = [[owin[q, c, h, rows, :] for c in range(2)] for q in range(2)]
                    for m in range(modes):
                        p_re = probe[0, m, rows, sides[h]]
                        p_im = probe[1, m, rows, sides[h]]
                        terms = []
                        for q in range(2):
                            w0, w1 = (v[m * BLOCK + at : m * BLOCK + at + CHUNK] for v in w[q])
                            chi = w0 + w1 if h == 0 else w0 - w1
                            c_re = chi[:, :half]
                            c_im = chi[:, half:]
                            t_re = p_re * c_re + p_im * c_im
                            t_im = p_re * c_im - p_im * c_re
                            g[q][0][h] = t_re if m == 0 else g[q][0][h] + t_re
                            g[q][1][h] = t_im if m == 0 else g[q][1][h] + t_im
                            o_re, o_im = o[q]
                            terms.append((o_re * c_re + o_im * c_im, o_re * c_im - o_im * c_re))
                        for c in range(2):
                            acc[c, m, rows, sides[h]] += terms[0][c] + terms[1][c]
                for q in range(2):
                    for c in range(2):
                        left = pltpu.roll(g[q][c][0], col[q], 1)
                        right = pltpu.roll(g[q][c][1], col[q], 1)
                        zero = jnp.zeros_like(left)
                        spread = (
                            jnp.where(keep_right[q], left, zero),
                            jnp.where(keep_right[q], right, left),
                            jnp.where(keep_right[q], zero, right),
                        )
                        for t in range(3):
                            sums[t][c, pl.ds(row[q] + rows.start, CHUNK), :] += spread[t]
        return 0

    lax.fori_loop(0, lax.div(live + 1, 2), pair_of_slots, 0)

    g_next[...] = mid[...].astype(BF16)
    for m in range(modes):
        for at in range(0, win, 8):
            for h in range(2):
                to = (m * win + at) * 2 + 8 * h
                acc_keep[to : to + 8, :] = acc[core, m, at : at + 8, h * LANES : (h + 1) * LANES]
            pair = acc[1 - core, m, at : at + 8, :]
            to = (m * win + at) * 2
            acc_send[to : to + 16, :] = jnp.concatenate([pair[:, :LANES], pair[:, LANES:]], axis=0).astype(BF16)


def prepare_kernel(fwd, bwd, perm, probe, meas, fwd_out, bwd_out, probe_out, meas_out, swaps, raw, sems):
    copies = [
        pltpu.make_async_copy(source, target, sems.at[i])
        for i, (source, target) in enumerate(
            ((perm, swaps), (meas.at[0], raw), (probe, probe_out), (fwd, fwd_out), (bwd, bwd_out))
        )
    ]
    for copy in copies:
        copy.start()
    copies[0].wait()
    copies[1].wait()
    for s in range(raw.shape[0]):
        rows_done = jnp.dot(swaps[0], raw[s], preferred_element_type=F32).astype(BF16)
        meas_out[s] = jnp.dot(rows_done, swaps[1], preferred_element_type=F32).astype(BF16)
    for copy in copies[2:]:
        copy.wait()


def prepare(probe, measured):
    slots, win = measured.shape[1:3]
    fwd, bwd, perm = dft_tables(win)
    return pl.pallas_call(
        prepare_kernel,
        in_specs=[pl.BlockSpec(memory_space=pltpu.HBM)] * 5,
        out_specs=[pl.BlockSpec(memory_space=pltpu.VMEM)] * 4,
        out_shape=[
            jax.ShapeDtypeStruct(fwd.shape, BF16),
            jax.ShapeDtypeStruct(bwd.shape, BF16),
            jax.ShapeDtypeStruct(probe.shape, F32),
            jax.ShapeDtypeStruct(measured.shape[1:], BF16),
        ],
        scratch_shapes=[
            pltpu.VMEM(perm.shape, BF16),
            pltpu.VMEM(measured.shape[1:], BF16),
            pltpu.SemaphoreType.DMA((5,)),
        ],
        cost_estimate=pl.CostEstimate(flops=4 * slots * win**3, bytes_accessed=8 << 20, transcendentals=0),
        compiler_params=pltpu.CompilerParams(vmem_limit_bytes=8 * 1024 * 1024),
        name="prepare",
    )(jnp.asarray(fwd), jnp.asarray(bwd), jnp.asarray(perm), probe, measured)


def run_slots(info, fwd, bwd, probe, measured, own, own_low, nxt, nxt_low, sec, sec_low):
    tile_rows, tile_cols = own.shape[1:]
    modes, win = probe.shape[1:3]
    tall = (2, tile_rows + win, tile_cols)
    flat = (2 * modes * win, LANES)
    blocks = (2, win // BLOCK, 2 * modes * BLOCK, win)
    vmem = pl.BlockSpec(memory_space=pltpu.VMEM)
    return pl.pallas_call(
        slots_kernel,
        in_specs=[pl.BlockSpec(memory_space=pltpu.SMEM)] + [vmem] * 10,
        out_specs=[vmem] * 5,
        out_shape=[
            jax.ShapeDtypeStruct(tall, F32),
            jax.ShapeDtypeStruct(tall, BF16),
            jax.ShapeDtypeStruct(tall, F32),
            jax.ShapeDtypeStruct(flat, F32),
            jax.ShapeDtypeStruct(flat, BF16),
        ],
        scratch_shapes=[
            pltpu.VMEM((2, 3) + tall[1:], F32),
            pltpu.VMEM(tall, F32),
            pltpu.VMEM((2, modes, win, win), F32),
            pltpu.VMEM((2, 2, 2, win, LANES), F32),
            pltpu.VMEM((2, modes, 2, win, win), BF16),
            pltpu.VMEM(blocks, BF16),
            pltpu.VMEM((2, modes, 2, win, win), BF16),
            pltpu.VMEM(blocks, BF16),
        ],
        compiler_params=pltpu.CompilerParams(vmem_limit_bytes=32 * 1024 * 1024),
        name="slots",
    )(info, fwd, bwd, probe, measured, own, own_low, nxt, nxt_low, sec, sec_low)


def moved(value, target):
    n_rows = lax.axis_size("rows")
    n_cols = lax.axis_size("cols")
    pairs = []
    for a in range(n_rows):
        for b in range(n_cols):
            to_a, to_b = target(a, b)
            if 0 <= to_a < n_rows and 0 <= to_b < n_cols:
                pairs.append((a * n_cols + b, to_a * n_cols + to_b))
    return lax.ppermute(value, ("rows", "cols"), pairs)


def swap_cores(value):
    return moved(value, lambda a, b: (a, b ^ 1))


def local(object_field, probe_mode_stack, measured, corner_row, corner_col, count):
    tile_rows, tile_cols = object_field.shape[1:]
    modes, win = probe_mode_stack.shape[1:3]
    slot_count = measured.shape[1]
    devices = lax.axis_size("rows") * lax.axis_size("cols")
    col_at = lax.axis_index("cols")
    core = lax.rem(col_at, 2)

    top = object_field[:, :win, :]
    sec = moved(object_field, lambda a, b: (a, b - 2))
    sec_low = moved(top, lambda a, b: (a - 1, b - 2))
    own_low = moved(top, lambda a, b: (a - 1, b))
    prepared, sec = lax.optimization_barrier((prepare(probe_mode_stack, measured), sec))
    nxt_low = swap_cores(jnp.where(core == 0, sec_low, own_low))
    nxt = swap_cores(jnp.where(core == 0, sec, object_field))
    info = jnp.concatenate(
        [
            corner_row[0] - lax.axis_index("rows") * tile_rows,
            corner_col[0] - col_at * tile_cols,
            count[0],
            core[None],
        ]
    )
    g_own, g_next, g_sec, acc_keep, acc_send = run_slots(
        info, *prepared, object_field, own_low, nxt, nxt_low, sec, sec_low
    )

    acc_got = swap_cores(acc_send)
    near = swap_cores(g_next)
    chip_sum = (acc_keep + acc_got.astype(F32)).astype(BF16)
    chip_sum, near = lax.optimization_barrier((chip_sum, near))
    near = lax.optimization_barrier(near.astype(F32))
    none = jnp.zeros_like(near)
    inner, near = lax.optimization_barrier((g_own + jnp.where(core == 1, near, none), near))
    outward = (g_sec + jnp.where(core == 0, near, none)).astype(BF16)
    far = moved(outward, lambda a, b: (a, b + 2))
    total = inner + far.astype(F32)
    rim = moved(total[:, tile_rows:].astype(BF16), lambda a, b: (a + 1, b))

    groups = [[i for i in range(devices) if i % 2 == c] for c in range(2)]
    exchange = functools.partial(
        lax.all_to_all, axis_name=("rows", "cols"), split_axis=0, concat_axis=0,
        axis_index_groups=groups, tiled=True,
    )
    share = exchange(chip_sum.reshape(devices // 2, -1, LANES))
    scale = 1.0 / jnp.sqrt(jnp.float32(devices * slot_count))
    share = (jnp.sum(share.astype(F32), axis=0) * scale).astype(BF16)
    mine = exchange(jnp.broadcast_to(share[None], (devices // 2,) + share.shape))
    mine, rim = lax.optimization_barrier((mine, rim))
    mine = mine.reshape(-1, LANES)
    part = lax.broadcasted_iota(jnp.int32, (2,) + mine.shape, 0)
    probe_grad = jnp.where(part == core, mine[None], swap_cores(mine)[None]).astype(F32)
    probe_grad = probe_grad.reshape(2, modes, win // 8, 2, 8, LANES).transpose(0, 1, 2, 4, 3, 5)
    probe_grad = probe_grad.reshape(2, modes, win, win)

    object_grad = total[:, :tile_rows] + jnp.pad(rim.astype(F32), ((0, 0), (0, tile_rows - win), (0, 0)))
    return (object_grad, probe_grad)


def solution(mesh):
    placed = (
        P(None, "rows", "cols"),
        P(),
        P("rows", "cols", None, None),
        P("rows", "cols"),
        P("rows", "cols"),
        P("rows", "cols"),
    )
    return jax.shard_map(
        local, mesh=mesh, in_specs=placed, out_specs=(P(None, "rows", "cols"), P()), check_vma=False
    )
```

```python
import functools

import jax
import jax.numpy as jnp
import ml_dtypes
import numpy as np
from jax import lax
from jax.experimental import pallas as pl
from jax.experimental.pallas import tpu as pltpu
from jax.sharding import PartitionSpec as P

F32 = jnp.float32
BF16 = jnp.bfloat16
LANES = 128
CHUNK = 16
BLOCK = 64


def dft_tables(win):
    half = win // 2
    k = np.arange(win)[:, None]
    j = np.arange(win)[None, :]
    angle = (k * j % win).astype(np.float64) * (2.0 * np.pi / win)
    re = np.cos(angle) / np.sqrt(win)
    im = -np.sin(angle) / np.sqrt(win)
    tables = []
    for parity in range(2):
        cr = re[parity::2, :half]
        ci = im[parity::2, :half]
        tables.append(np.block([[cr, -ci], [ci, cr]]))
    forward = np.stack(tables)
    backward = np.stack([t.T for t in tables])
    order = np.concatenate([np.arange(0, win, 2), np.arange(1, win, 2)])
    permute = np.zeros((win, win))
    permute[np.arange(win), order] = 1.0
    both = np.stack([permute, permute.T])
    cast = lambda a: a.astype(ml_dtypes.bfloat16)
    return cast(forward), cast(backward), cast(both)


def slots_kernel(
    info, fwd, bwd, probe, meas, own, own_low, nxt, nxt_low, sec, sec_low,
    g_own, g_next, g_next_low, g_sec, acc_keep, acc_send,
    ext, mid, acc, owin, xs, hb, gb, kb,
):
    slots = meas.shape[0]
    live = info[2 * slots]
    core = info[2 * slots + 1]
    modes = probe.shape[1]
    win = probe.shape[2]
    half = win // 2
    blocks = win // BLOCK
    tile_rows = own.shape[1]
    sums = (g_own, mid, g_sec)

    for c in range(2):
        for t, (top, bottom) in enumerate(((own, own_low), (nxt, nxt_low), (sec, sec_low))):
            ext[c, t, :tile_rows, :] = top[c].astype(F32)
            ext[c, t, tile_rows:, :] = bottom[c].astype(F32)
    for ref in sums + (acc,):
        ref[...] = jnp.zeros_like(ref)

    sides = (slice(0, LANES), slice(LANES, 2 * LANES))
    lane = lax.broadcasted_iota(jnp.int32, (CHUNK, LANES), 1)

    def pair_of_slots(pair, _):
        whole = 2 * pair + 1 < live
        slot = (2 * pair, jnp.where(whole, 2 * pair + 1, 2 * pair))
        weight = (None, jnp.where(whole, 1.0, 0.0).astype(F32))
        row = [info[s] for s in slot]
        col = [info[slots + s] for s in slot]
        left_shift = [lax.rem(LANES - c, LANES) for c in col]
        keep_left = [lane < LANES - c for c in col]
        keep_right = [lane >= c for c in col]

        for q in range(2):
            for at in range(0, win, CHUNK):
                for c in range(2):
                    parts = [
                        pltpu.roll(ext[c, t, pl.ds(row[q] + at, CHUNK), :], left_shift[q], 1) for t in range(3)
                    ]
                    for h in range(2):
                        owin[q, c, h, at : at + CHUNK, :] = jnp.where(keep_left[q], parts[h], parts[h + 1])

        for m in range(modes):
            for at in range(0, half, CHUNK):
                for h in range(2):
                    psi = ([], [])
                    for rows in (slice(at, at + CHUNK), slice(half + at, half + at + CHUNK)):
                        p_re = probe[0, m, rows, sides[h]]
                        p_im = probe[1, m, rows, sides[h]]
                        for q in range(2):
                            o_re = owin[q, 0, h, rows, :]
                            o_im = owin[q, 1, h, rows, :]
                            psi[q].append((p_re * o_re - p_im * o_im, p_re * o_im + p_im * o_re))
                    for q in range(2):
                        for c in range(2):
                            rows = slice(c * half + at, c * half + at + CHUNK)
                            xs[q, m, 0, rows, sides[h]] = (psi[q][0][c] + psi[q][1][c]).astype(BF16)
                            xs[q, m, 1, rows, sides[h]] = (psi[q][0][c] - psi[q][1][c]).astype(BF16)
            for q in range(2):
                for rp in range(2):
                    v = jnp.dot(fwd[rp], xs[q, m, rp], preferred_element_type=F32)
                    v = (
                        (v[:, :half] + v[:, half:]).astype(BF16),
                        (v[:, :half] - v[:, half:]).astype(BF16),
                    )
                    for pc in range(2):
                        for at in range(0, half, BLOCK):
                            for c in range(2):
                                first = (q * modes + m) * BLOCK
                                hb[pc, (rp * half + at) // BLOCK, first : first + BLOCK, sides[c]] = v[pc][c * half + at : c * half + at + BLOCK]

        for rb in range(blocks):
            for pc in range(2):
                fields = jnp.dot(hb[pc, rb], bwd[pc], preferred_element_type=F32)
                for q in range(2):
                    field = fields[q * modes * BLOCK : (q + 1) * modes * BLOCK]
                    for at in range(0, BLOCK, CHUNK):
                        part = [field[m * BLOCK + at : m * BLOCK + at + CHUNK] for m in range(modes)]
                        total = 1.0
                        for f in part:
                            total = total + (f[:, :half] * f[:, :half] + f[:, half:] * f[:, half:])
                        f_row = rb * BLOCK + at
                        factor = 1.0 - meas[slot[q], f_row : f_row + CHUNK, sides[pc]].astype(F32) * lax.rsqrt(total)
                        if q == 1:
                            factor = factor * weight[q]
                        rp, f_row = divmod(f_row, half)
                        for m in range(modes):
                            for c in range(2):
                                gb[q, m, rp, c * half + f_row : c * half + f_row + CHUNK, sides[pc]] = (
                                    part[m][:, sides[c]] * factor
                                ).astype(BF16)

        for m in range(modes):
            for q in range(2):
                v0 = jnp.dot(bwd[0], gb[q, m, 0], preferred_element_type=F32)
                v1 = jnp.dot(bwd[1], gb[q, m, 1], preferred_element_type=F32)
                for side, v in enumerate(((v0 + v1).astype(BF16), (v0 - v1).astype(BF16))):
                    for at in range(0, half, BLOCK):
                        for pc in range(2):
                            for c in range(2):
                                first = (q * modes + m) * BLOCK
                                kb[pc, (side * half + at) // BLOCK, first : first + BLOCK, sides[c]] = v[c * half + at : c * half + at + BLOCK, sides[pc]]

        for rb in range(blocks):
            fields = [jnp.dot(kb[pc, rb], fwd[pc], preferred_element_type=F32) for pc in range(2)]
            w = [[f[q * modes * BLOCK : (q + 1) * modes * BLOCK] for f in fields] for q in range(2)]
            for at in range(0, BLOCK, CHUNK):
                rows = slice(rb * BLOCK + at, rb * BLOCK + at + CHUNK)
                g = [[[None, None], [None, None]] for q in range(2)]
                for h in range(2):
                    o = [[owin[q, c, h, rows, :] for c in range(2)] for q in range(2)]
                    for m in range(modes):
                        p_re = probe[0, m, rows, sides[h]]
                        p_im = probe[1, m, rows, sides[h]]
                        terms = []
                        for q in range(2):
                            w0, w1 = (v[m * BLOCK + at : m * BLOCK + at + CHUNK] for v in w[q])
                            chi = w0 + w1 if h == 0 else w0 - w1
                            c_re = chi[:, :half]
                            c_im = chi[:, half:]
                            t_re = p_re * c_re + p_im * c_im
                            t_im = p_re * c_im - p_im * c_re
                            g[q][0][h] = t_re if m == 0 else g[q][0][h] + t_re
                            g[q][1][h] = t_im if m == 0 else g[q][1][h] + t_im
                            o_re, o_im = o[q]
                            terms.append((o_re * c_re + o_im * c_im, o_re * c_im - o_im * c_re))
                        for c in range(2):
                            acc[c, m, rows, sides[h]] += terms[0][c] + terms[1][c]
                for q in range(2):
                    for c in range(2):
                        left = pltpu.roll(g[q][c][0], col[q], 1)
                        right = pltpu.roll(g[q][c][1], col[q], 1)
                        zero = jnp.zeros_like(left)
                        spread = (
                            jnp.where(keep_right[q], left, zero),
                            jnp.where(keep_right[q], right, left),
                            jnp.where(keep_right[q], zero, right),
                        )
                        for t in range(3):
                            sums[t][c, pl.ds(row[q] + rows.start, CHUNK), :] += spread[t]
        return 0

    lax.fori_loop(0, lax.div(live + 1, 2), pair_of_slots, 0)

    g_next[...] = mid[:, :tile_rows, :].astype(BF16)
    g_next_low[...] = mid[:, tile_rows:, :].astype(BF16)
    for m in range(modes):
        for at in range(0, win, 8):
            for h in range(2):
                to = (m * win + at) * 2 + 8 * h
                acc_keep[to : to + 8, :] = acc[core, m, at : at + 8, h * LANES : (h + 1) * LANES]
            pair = acc[1 - core, m, at : at + 8, :]
            to = (m * win + at) * 2
            acc_send[to : to + 16, :] = jnp.concatenate([pair[:, :LANES], pair[:, LANES:]], axis=0).astype(BF16)


def prepare_kernel(fwd, bwd, perm, probe, meas, fwd_out, bwd_out, probe_out, meas_out, swaps, raw, sems):
    copies = [
        pltpu.make_async_copy(source, target, sems.at[i])
        for i, (source, target) in enumerate(
            ((perm, swaps), (meas.at[0], raw), (probe, probe_out), (fwd, fwd_out), (bwd, bwd_out))
        )
    ]
    for copy in copies:
        copy.start()
    copies[0].wait()
    copies[1].wait()
    for s in range(raw.shape[0]):
        rows_done = jnp.dot(swaps[0], raw[s], preferred_element_type=F32).astype(BF16)
        meas_out[s] = jnp.dot(rows_done, swaps[1], preferred_element_type=F32).astype(BF16)
    for copy in copies[2:]:
        copy.wait()


def prepare(probe, measured):
    slots, win = measured.shape[1:3]
    fwd, bwd, perm = dft_tables(win)
    return pl.pallas_call(
        prepare_kernel,
        in_specs=[pl.BlockSpec(memory_space=pltpu.HBM)] * 5,
        out_specs=[pl.BlockSpec(memory_space=pltpu.VMEM)] * 4,
        out_shape=[
            jax.ShapeDtypeStruct(fwd.shape, BF16),
            jax.ShapeDtypeStruct(bwd.shape, BF16),
            jax.ShapeDtypeStruct(probe.shape, F32),
            jax.ShapeDtypeStruct(measured.shape[1:], BF16),
        ],
        scratch_shapes=[
            pltpu.VMEM(perm.shape, BF16),
            pltpu.VMEM(measured.shape[1:], BF16),
            pltpu.SemaphoreType.DMA((5,)),
        ],
        cost_estimate=pl.CostEstimate(flops=4 * slots * win**3, bytes_accessed=8 << 20, transcendentals=0),
        compiler_params=pltpu.CompilerParams(vmem_limit_bytes=8 * 1024 * 1024),
        name="prepare",
    )(jnp.asarray(fwd), jnp.asarray(bwd), jnp.asarray(perm), probe, measured)


def run_slots(info, fwd, bwd, probe, measured, own, own_low, nxt, nxt_low, sec, sec_low):
    tile_rows, tile_cols = own.shape[1:]
    modes, win = probe.shape[1:3]
    tall = (2, tile_rows + win, tile_cols)
    flat = (2 * modes * win, LANES)
    blocks = (2, win // BLOCK, 2 * modes * BLOCK, win)
    vmem = pl.BlockSpec(memory_space=pltpu.VMEM)
    return pl.pallas_call(
        slots_kernel,
        in_specs=[pl.BlockSpec(memory_space=pltpu.SMEM)] + [vmem] * 10,
        out_specs=[vmem] * 6,
        out_shape=[
            jax.ShapeDtypeStruct(tall, F32),
            jax.ShapeDtypeStruct(own.shape, BF16),
            jax.ShapeDtypeStruct(own_low.shape, BF16),
            jax.ShapeDtypeStruct(tall, F32),
            jax.ShapeDtypeStruct(flat, F32),
            jax.ShapeDtypeStruct(flat, BF16),
        ],
        scratch_shapes=[
            pltpu.VMEM((2, 3) + tall[1:], F32),
            pltpu.VMEM(tall, F32),
            pltpu.VMEM((2, modes, win, win), F32),
            pltpu.VMEM((2, 2, 2, win, LANES), F32),
            pltpu.VMEM((2, modes, 2, win, win), BF16),
            pltpu.VMEM(blocks, BF16),
            pltpu.VMEM((2, modes, 2, win, win), BF16),
            pltpu.VMEM(blocks, BF16),
        ],
        compiler_params=pltpu.CompilerParams(vmem_limit_bytes=22 * 1024 * 1024),
        name="slots",
    )(info, fwd, bwd, probe, measured, own, own_low, nxt, nxt_low, sec, sec_low)


def share_kernel(scale, parts, out):
    total = parts[0].astype(F32)
    for i in range(1, parts.shape[0]):
        total = total + parts[i].astype(F32)
    total = (total * scale).astype(BF16)
    for i in range(out.shape[0]):
        out[i] = total


def share_out(parts, scale):
    vmem = pl.BlockSpec(memory_space=pltpu.VMEM)
    return pl.pallas_call(
        functools.partial(share_kernel, scale),
        in_specs=[vmem],
        out_specs=vmem,
        out_shape=jax.ShapeDtypeStruct(parts.shape, BF16),
        compiler_params=pltpu.CompilerParams(vmem_limit_bytes=4 * 1024 * 1024),
        name="share",
    )(parts)


def moved(value, target):
    n_rows = lax.axis_size("rows")
    n_cols = lax.axis_size("cols")
    pairs = []
    for a in range(n_rows):
        for b in range(n_cols):
            to_a, to_b = target(a, b)
            if 0 <= to_a < n_rows and 0 <= to_b < n_cols:
                pairs.append((a * n_cols + b, to_a * n_cols + to_b))
    return lax.ppermute(value, ("rows", "cols"), pairs)


def swap_cores(value):
    return moved(value, lambda a, b: (a, b ^ 1))


def local(object_field, probe_mode_stack, measured, corner_row, corner_col, count):
    tile_rows, tile_cols = object_field.shape[1:]
    modes, win = probe_mode_stack.shape[1:3]
    slot_count = measured.shape[1]
    devices = lax.axis_size("rows") * lax.axis_size("cols")
    col_at = lax.axis_index("cols")
    core = lax.rem(col_at, 2)

    top = object_field[:, :win, :]
    sec = moved(object_field, lambda a, b: (a, b - 2))
    sec_low = moved(top, lambda a, b: (a - 1, b - 2))
    own_low = moved(top, lambda a, b: (a - 1, b))
    prepared, sec = lax.optimization_barrier((prepare(probe_mode_stack, measured), sec))
    nxt_low = swap_cores(jnp.where(core == 0, sec_low, own_low))
    nxt = swap_cores(jnp.where(core == 0, sec, object_field))
    info = jnp.concatenate(
        [
            corner_row[0] - lax.axis_index("rows") * tile_rows,
            corner_col[0] - col_at * tile_cols,
            count[0],
            core[None],
        ]
    )
    g_own, g_next, g_next_low, g_sec, acc_keep, acc_send = run_slots(
        info, *prepared, object_field, own_low, nxt, nxt_low, sec, sec_low
    )

    acc_got = swap_cores(acc_send)
    near = swap_cores(g_next)
    chip_sum = (acc_keep + acc_got.astype(F32)).astype(BF16)
    near, near_low = lax.optimization_barrier((near, g_next_low))
    near = jnp.concatenate([near, swap_cores(near_low)], axis=1).astype(F32)
    none = jnp.zeros_like(near)
    outward = (g_sec + jnp.where(core == 0, near, none)).astype(BF16)
    far = moved(outward, lambda a, b: (a, b + 2))
    total = g_own + jnp.where(core == 1, near, none) + far.astype(F32)
    rim = moved(total[:, tile_rows:].astype(BF16), lambda a, b: (a + 1, b))

    groups = [[i for i in range(devices) if i % 2 == c] for c in range(2)]
    exchange = functools.partial(
        lax.all_to_all, axis_name=("rows", "cols"), split_axis=0, concat_axis=0,
        axis_index_groups=groups, tiled=True,
    )
    share = exchange(chip_sum.reshape(devices // 2, -1, LANES))
    mine = exchange(share_out(share, 1.0 / float(np.sqrt(devices * slot_count))))
    mine, rim = lax.optimization_barrier((mine, rim))
    mine = mine.reshape(-1, LANES)
    part = lax.broadcasted_iota(jnp.int32, (2,) + mine.shape, 0)
    probe_grad = jnp.where(part == core, mine[None], swap_cores(mine)[None]).astype(F32)
    probe_grad = probe_grad.reshape(2, modes, win // 8, 2, 8, LANES).transpose(0, 1, 2, 4, 3, 5)
    probe_grad = probe_grad.reshape(2, modes, win, win)

    object_grad = total[:, :tile_rows] + jnp.pad(rim.astype(F32), ((0, 0), (0, tile_rows - win), (0, 0)))
    return (object_grad, probe_grad)


def solution(mesh):
    placed = (
        P(None, "rows", "cols"),
        P(),
        P("rows", "cols", None, None),
        P("rows", "cols"),
        P("rows", "cols"),
        P("rows", "cols"),
    )
    return jax.shard_map(
        local, mesh=mesh, in_specs=placed, out_specs=(P(None, "rows", "cols"), P()), check_vma=False
    )
```

```python
import functools

import jax
import jax.numpy as jnp
import ml_dtypes
import numpy as np
from jax import lax
from jax.experimental import pallas as pl
from jax.experimental.pallas import tpu as pltpu
from jax.sharding import PartitionSpec as P

F32 = jnp.float32
BF16 = jnp.bfloat16
LANES = 128
CHUNK = 16
BLOCK = 64


def dft_tables(win):
    half = win // 2
    k = np.arange(win)[:, None]
    j = np.arange(win)[None, :]
    angle = (k * j % win).astype(np.float64) * (2.0 * np.pi / win)
    re = np.cos(angle) / np.sqrt(win)
    im = -np.sin(angle) / np.sqrt(win)
    tables = []
    for parity in range(2):
        cr = re[parity::2, :half]
        ci = im[parity::2, :half]
        tables.append(np.block([[cr, -ci], [ci, cr]]))
    forward = np.stack(tables)
    backward = np.stack([t.T for t in tables])
    order = np.concatenate([np.arange(0, win, 2), np.arange(1, win, 2)])
    permute = np.zeros((win, win))
    permute[np.arange(win), order] = 1.0
    both = np.stack([permute, permute.T])
    cast = lambda a: a.astype(ml_dtypes.bfloat16)
    return cast(forward), cast(backward), cast(both)


def slots_kernel(
    info, fwd, bwd, probe, meas, own, own_low, nxt, nxt_low, sec, sec_low,
    g_own, g_next, g_next_low, g_sec, acc_keep, acc_send,
    ext, mid, acc, owin, xs, hb, gb, kb,
):
    slots = meas.shape[0]
    live = info[2 * slots]
    core = info[2 * slots + 1]
    modes = probe.shape[1]
    win = probe.shape[2]
    half = win // 2
    blocks = win // BLOCK
    tile_rows = own.shape[1]
    sums = (g_own, mid, g_sec)

    for c in range(2):
        for t, (top, bottom) in enumerate(((own, own_low), (nxt, nxt_low), (sec, sec_low))):
            ext[c, t, :tile_rows, :] = top[c].astype(F32)
            ext[c, t, tile_rows:, :] = bottom[c].astype(F32)
    for ref in sums + (acc,):
        ref[...] = jnp.zeros_like(ref)

    sides = (slice(0, LANES), slice(LANES, 2 * LANES))
    lane = lax.broadcasted_iota(jnp.int32, (CHUNK, LANES), 1)

    def pair_of_slots(pair, _):
        whole = 2 * pair + 1 < live
        slot = (2 * pair, jnp.where(whole, 2 * pair + 1, 2 * pair))
        weight = (None, jnp.where(whole, 1.0, 0.0).astype(F32))
        row = [info[s] for s in slot]
        col = [info[slots + s] for s in slot]
        left_shift = [lax.rem(LANES - c, LANES) for c in col]
        keep_left = [lane < LANES - c for c in col]
        keep_right = [lane >= c for c in col]

        for q in range(2):
            for at in range(0, win, CHUNK):
                for c in range(2):
                    parts = [
                        pltpu.roll(ext[c, t, pl.ds(row[q] + at, CHUNK), :], left_shift[q], 1) for t in range(3)
                    ]
                    for h in range(2):
                        owin[q, c, h, at : at + CHUNK, :] = jnp.where(keep_left[q], parts[h], parts[h + 1])

        for m in range(modes):
            for at in range(0, half, CHUNK):
                for h in range(2):
                    psi = ([], [])
                    for rows in (slice(at, at + CHUNK), slice(half + at, half + at + CHUNK)):
                        p_re = probe[0, m, rows, sides[h]]
                        p_im = probe[1, m, rows, sides[h]]
                        for q in range(2):
                            o_re = owin[q, 0, h, rows, :]
                            o_im = owin[q, 1, h, rows, :]
                            psi[q].append((p_re * o_re - p_im * o_im, p_re * o_im + p_im * o_re))
                    for q in range(2):
                        for c in range(2):
                            rows = slice(c * half + at, c * half + at + CHUNK)
                            xs[q, m, 0, rows, sides[h]] = (psi[q][0][c] + psi[q][1][c]).astype(BF16)
                            xs[q, m, 1, rows, sides[h]] = (psi[q][0][c] - psi[q][1][c]).astype(BF16)
            for q in range(2):
                for rp in range(2):
                    v = jnp.dot(fwd[rp], xs[q, m, rp], preferred_element_type=F32)
                    v = (
                        (v[:, :half] + v[:, half:]).astype(BF16),
                        (v[:, :half] - v[:, half:]).astype(BF16),
                    )
                    for pc in range(2):
                        for at in range(0, half, BLOCK):
                            for c in range(2):
                                first = (q * modes + m) * BLOCK
                                hb[pc, (rp * half + at) // BLOCK, first : first + BLOCK, sides[c]] = v[pc][c * half + at : c * half + at + BLOCK]

        for rb in range(blocks):
            for pc in range(2):
                fields = jnp.dot(hb[pc, rb], bwd[pc], preferred_element_type=F32)
                for q in range(2):
                    field = fields[q * modes * BLOCK : (q + 1) * modes * BLOCK]
                    for at in range(0, BLOCK, CHUNK):
                        part = [field[m * BLOCK + at : m * BLOCK + at + CHUNK] for m in range(modes)]
                        total = 1.0
                        for f in part:
                            total = total + (f[:, :half] * f[:, :half] + f[:, half:] * f[:, half:])
                        f_row = rb * BLOCK + at
                        factor = 1.0 - meas[slot[q], f_row : f_row + CHUNK, sides[pc]].astype(F32) * lax.rsqrt(total)
                        if q == 1:
                            factor = factor * weight[q]
                        rp, f_row = divmod(f_row, half)
                        for m in range(modes):
                            for c in range(2):
                                gb[q, m, rp, c * half + f_row : c * half + f_row + CHUNK, sides[pc]] = (
                                    part[m][:, sides[c]] * factor
                                ).astype(BF16)

        for m in range(modes):
            for q in range(2):
                v0 = jnp.dot(bwd[0], gb[q, m, 0], preferred_element_type=F32)
                v1 = jnp.dot(bwd[1], gb[q, m, 1], preferred_element_type=F32)
                for side, v in enumerate(((v0 + v1).astype(BF16), (v0 - v1).astype(BF16))):
                    for at in range(0, half, BLOCK):
                        for pc in range(2):
                            for c in range(2):
                                first = (q * modes + m) * BLOCK
                                kb[pc, (side * half + at) // BLOCK, first : first + BLOCK, sides[c]] = v[c * half + at : c * half + at + BLOCK, sides[pc]]

        for rb in range(blocks):
            fields = [jnp.dot(kb[pc, rb], fwd[pc], preferred_element_type=F32) for pc in range(2)]
            w = [[f[q * modes * BLOCK : (q + 1) * modes * BLOCK] for f in fields] for q in range(2)]
            for at in range(0, BLOCK, CHUNK):
                rows = slice(rb * BLOCK + at, rb * BLOCK + at + CHUNK)
                g = [[[None, None], [None, None]] for q in range(2)]
                for h in range(2):
                    o = [[owin[q, c, h, rows, :] for c in range(2)] for q in range(2)]
                    for m in range(modes):
                        p_re = probe[0, m, rows, sides[h]]
                        p_im = probe[1, m, rows, sides[h]]
                        terms = []
                        for q in range(2):
                            w0, w1 = (v[m * BLOCK + at : m * BLOCK + at + CHUNK] for v in w[q])
                            chi = w0 + w1 if h == 0 else w0 - w1
                            c_re = chi[:, :half]
                            c_im = chi[:, half:]
                            t_re = p_re * c_re + p_im * c_im
                            t_im = p_re * c_im - p_im * c_re
                            g[q][0][h] = t_re if m == 0 else g[q][0][h] + t_re
                            g[q][1][h] = t_im if m == 0 else g[q][1][h] + t_im
                            o_re, o_im = o[q]
                            terms.append((o_re * c_re + o_im * c_im, o_re * c_im - o_im * c_re))
                        for c in range(2):
                            acc[c, m, rows, sides[h]] += terms[0][c] + terms[1][c]
                for q in range(2):
                    for c in range(2):
                        left = pltpu.roll(g[q][c][0], col[q], 1)
                        right = pltpu.roll(g[q][c][1], col[q], 1)
                        zero = jnp.zeros_like(left)
                        spread = (
                            jnp.where(keep_right[q], left, zero),
                            jnp.where(keep_right[q], right, left),
                            jnp.where(keep_right[q], zero, right),
                        )
                        for t in range(3):
                            sums[t][c, pl.ds(row[q] + rows.start, CHUNK), :] += spread[t]
        return 0

    lax.fori_loop(0, lax.div(live + 1, 2), pair_of_slots, 0)

    g_next[...] = mid[:, :tile_rows, :].astype(BF16)
    g_next_low[...] = mid[:, tile_rows:, :].astype(BF16)
    for m in range(modes):
        for at in range(0, win, 8):
            for h in range(2):
                to = (m * win + at) * 2 + 8 * h
                acc_keep[to : to + 8, :] = acc[core, m, at : at + 8, h * LANES : (h + 1) * LANES]
            pair = acc[1 - core, m, at : at + 8, :]
            to = (m * win + at) * 2
            acc_send[to : to + 16, :] = jnp.concatenate([pair[:, :LANES], pair[:, LANES:]], axis=0).astype(BF16)


def prepare_kernel(fwd, bwd, perm, probe, meas, fwd_out, bwd_out, probe_out, meas_out, swaps, raw, sems):
    copies = [
        pltpu.make_async_copy(source, target, sems.at[i])
        for i, (source, target) in enumerate(
            ((perm, swaps), (meas.at[0], raw), (probe, probe_out), (fwd, fwd_out), (bwd, bwd_out))
        )
    ]
    for copy in copies:
        copy.start()
    copies[0].wait()
    copies[1].wait()
    for s in range(raw.shape[0]):
        rows_done = jnp.dot(swaps[0], raw[s], preferred_element_type=F32).astype(BF16)
        meas_out[s] = jnp.dot(rows_done, swaps[1], preferred_element_type=F32).astype(BF16)
    for copy in copies[2:]:
        copy.wait()


def prepare(probe, measured):
    slots, win = measured.shape[1:3]
    fwd, bwd, perm = dft_tables(win)
    return pl.pallas_call(
        prepare_kernel,
        in_specs=[pl.BlockSpec(memory_space=pltpu.HBM)] * 5,
        out_specs=[pl.BlockSpec(memory_space=pltpu.VMEM)] * 4,
        out_shape=[
            jax.ShapeDtypeStruct(fwd.shape, BF16),
            jax.ShapeDtypeStruct(bwd.shape, BF16),
            jax.ShapeDtypeStruct(probe.shape, F32),
            jax.ShapeDtypeStruct(measured.shape[1:], BF16),
        ],
        scratch_shapes=[
            pltpu.VMEM(perm.shape, BF16),
            pltpu.VMEM(measured.shape[1:], BF16),
            pltpu.SemaphoreType.DMA((5,)),
        ],
        cost_estimate=pl.CostEstimate(flops=4 * slots * win**3, bytes_accessed=8 << 20, transcendentals=0),
        compiler_params=pltpu.CompilerParams(vmem_limit_bytes=8 * 1024 * 1024),
        name="prepare",
    )(jnp.asarray(fwd), jnp.asarray(bwd), jnp.asarray(perm), probe, measured)


def run_slots(info, fwd, bwd, probe, measured, own, own_low, nxt, nxt_low, sec, sec_low):
    tile_rows, tile_cols = own.shape[1:]
    modes, win = probe.shape[1:3]
    tall = (2, tile_rows + win, tile_cols)
    flat = (2 * modes * win, LANES)
    blocks = (2, win // BLOCK, 2 * modes * BLOCK, win)
    vmem = pl.BlockSpec(memory_space=pltpu.VMEM)
    return pl.pallas_call(
        slots_kernel,
        in_specs=[pl.BlockSpec(memory_space=pltpu.SMEM)] + [vmem] * 10,
        out_specs=[vmem] * 6,
        out_shape=[
            jax.ShapeDtypeStruct(tall, F32),
            jax.ShapeDtypeStruct(own.shape, BF16),
            jax.ShapeDtypeStruct(own_low.shape, BF16),
            jax.ShapeDtypeStruct(tall, F32),
            jax.ShapeDtypeStruct(flat, F32),
            jax.ShapeDtypeStruct(flat, BF16),
        ],
        scratch_shapes=[
            pltpu.VMEM((2, 3) + tall[1:], F32),
            pltpu.VMEM(tall, F32),
            pltpu.VMEM((2, modes, win, win), F32),
            pltpu.VMEM((2, 2, 2, win, LANES), F32),
            pltpu.VMEM((2, modes, 2, win, win), BF16),
            pltpu.VMEM(blocks, BF16),
            pltpu.VMEM((2, modes, 2, win, win), BF16),
            pltpu.VMEM(blocks, BF16),
        ],
        compiler_params=pltpu.CompilerParams(vmem_limit_bytes=22 * 1024 * 1024),
        name="slots",
    )(info, fwd, bwd, probe, measured, own, own_low, nxt, nxt_low, sec, sec_low)


def share_kernel(scale, parts, out):
    total = parts[0].astype(F32)
    for i in range(1, parts.shape[0]):
        total = total + parts[i].astype(F32)
    total = (total * scale).astype(BF16)
    for i in range(out.shape[0]):
        out[i] = total


def share_out(parts, scale):
    vmem = pl.BlockSpec(memory_space=pltpu.VMEM)
    return pl.pallas_call(
        functools.partial(share_kernel, scale),
        in_specs=[vmem],
        out_specs=vmem,
        out_shape=jax.ShapeDtypeStruct(parts.shape, BF16),
        cost_estimate=pl.CostEstimate(flops=0, bytes_accessed=128 << 20, transcendentals=0),
        compiler_params=pltpu.CompilerParams(vmem_limit_bytes=4 * 1024 * 1024),
        name="share",
    )(parts)


def moved(value, target):
    n_rows = lax.axis_size("rows")
    n_cols = lax.axis_size("cols")
    pairs = []
    for a in range(n_rows):
        for b in range(n_cols):
            to_a, to_b = target(a, b)
            if 0 <= to_a < n_rows and 0 <= to_b < n_cols:
                pairs.append((a * n_cols + b, to_a * n_cols + to_b))
    return lax.ppermute(value, ("rows", "cols"), pairs)


def swap_cores(value):
    return moved(value, lambda a, b: (a, b ^ 1))


def local(object_field, probe_mode_stack, measured, corner_row, corner_col, count):
    tile_rows, tile_cols = object_field.shape[1:]
    modes, win = probe_mode_stack.shape[1:3]
    slot_count = measured.shape[1]
    devices = lax.axis_size("rows") * lax.axis_size("cols")
    col_at = lax.axis_index("cols")
    core = lax.rem(col_at, 2)

    top = object_field[:, :win, :]
    sec = moved(object_field, lambda a, b: (a, b - 2))
    sec_low = moved(top, lambda a, b: (a - 1, b - 2))
    own_low = moved(top, lambda a, b: (a - 1, b))
    prepared, sec = lax.optimization_barrier((prepare(probe_mode_stack, measured), sec))
    nxt_low = swap_cores(jnp.where(core == 0, sec_low, own_low))
    nxt = swap_cores(jnp.where(core == 0, sec, object_field))
    info = jnp.concatenate(
        [
            corner_row[0] - lax.axis_index("rows") * tile_rows,
            corner_col[0] - col_at * tile_cols,
            count[0],
            core[None],
        ]
    )
    g_own, g_next, g_next_low, g_sec, acc_keep, acc_send = run_slots(
        info, *prepared, object_field, own_low, nxt, nxt_low, sec, sec_low
    )

    acc_got = swap_cores(acc_send)
    near = swap_cores(g_next)
    chip_sum = (acc_keep + acc_got.astype(F32)).astype(BF16)
    near, near_low = lax.optimization_barrier((near, g_next_low))
    near = jnp.concatenate([near, swap_cores(near_low)], axis=1).astype(F32)
    none = jnp.zeros_like(near)
    outward = (g_sec + jnp.where(core == 0, near, none)).astype(BF16)
    far = moved(outward, lambda a, b: (a, b + 2))
    total = g_own + jnp.where(core == 1, near, none) + far.astype(F32)
    rim = moved(total[:, tile_rows:].astype(BF16), lambda a, b: (a + 1, b))

    groups = [[i for i in range(devices) if i % 2 == c] for c in range(2)]
    exchange = functools.partial(
        lax.all_to_all, axis_name=("rows", "cols"), split_axis=0, concat_axis=0,
        axis_index_groups=groups, tiled=True,
    )
    share = exchange(chip_sum.reshape(devices // 2, -1, LANES))
    mine = exchange(share_out(share, 1.0 / float(np.sqrt(devices * slot_count))))
    mine, rim = lax.optimization_barrier((mine, rim))
    mine = mine.reshape(-1, LANES)
    part = lax.broadcasted_iota(jnp.int32, (2,) + mine.shape, 0)
    probe_grad = jnp.where(part == core, mine[None], swap_cores(mine)[None]).astype(F32)
    probe_grad = probe_grad.reshape(2, modes, win // 8, 2, 8, LANES).transpose(0, 1, 2, 4, 3, 5)
    probe_grad = probe_grad.reshape(2, modes, win, win)

    object_grad = total[:, :tile_rows] + jnp.pad(rim.astype(F32), ((0, 0), (0, tile_rows - win), (0, 0)))
    return (object_grad, probe_grad)


def solution(mesh):
    placed = (
        P(None, "rows", "cols"),
        P(),
        P("rows", "cols", None, None),
        P("rows", "cols"),
        P("rows", "cols"),
        P("rows", "cols"),
    )
    return jax.shard_map(
        local, mesh=mesh, in_specs=placed, out_specs=(P(None, "rows", "cols"), P()), check_vma=False
    )
```

```python
import functools

import jax
import jax.numpy as jnp
import ml_dtypes
import numpy as np
from jax import lax
from jax.experimental import pallas as pl
from jax.experimental.pallas import tpu as pltpu
from jax.sharding import PartitionSpec as P

F32 = jnp.float32
BF16 = jnp.bfloat16
LANES = 128
CHUNK = 16
BLOCK = 64


def dft_tables(win):
    half = win // 2
    k = np.arange(win)[:, None]
    j = np.arange(win)[None, :]
    angle = (k * j % win).astype(np.float64) * (2.0 * np.pi / win)
    re = np.cos(angle) / np.sqrt(win)
    im = -np.sin(angle) / np.sqrt(win)
    tables = []
    for parity in range(2):
        cr = re[parity::2, :half]
        ci = im[parity::2, :half]
        tables.append(np.block([[cr, -ci], [ci, cr]]))
    forward = np.stack(tables)
    backward = np.stack([t.T for t in tables])
    order = np.concatenate([np.arange(0, win, 2), np.arange(1, win, 2)])
    permute = np.zeros((win, win))
    permute[np.arange(win), order] = 1.0
    both = np.stack([permute, permute.T])
    cast = lambda a: a.astype(ml_dtypes.bfloat16)
    return cast(forward), cast(backward), cast(both)


def slots_kernel(
    info, fwd, bwd, probe, meas, own, own_low, nxt, nxt_low, sec, sec_low,
    g_own, g_next, g_next_low, g_sec, acc_keep, acc_send,
    ext, mid, acc, owin, xs, hb, gb, kb,
):
    slots = meas.shape[0]
    live = info[2 * slots]
    core = info[2 * slots + 1]
    modes = probe.shape[1]
    win = probe.shape[2]
    half = win // 2
    blocks = win // BLOCK
    tile_rows = own.shape[1]
    sums = (g_own, mid, g_sec)

    for c in range(2):
        for t, (top, bottom) in enumerate(((own, own_low), (nxt, nxt_low), (sec, sec_low))):
            ext[c, t, :tile_rows, :] = top[c].astype(F32)
            ext[c, t, tile_rows:, :] = bottom[c].astype(F32)
    for ref in sums + (acc,):
        ref[...] = jnp.zeros_like(ref)

    sides = (slice(0, LANES), slice(LANES, 2 * LANES))
    lane = lax.broadcasted_iota(jnp.int32, (CHUNK, LANES), 1)

    def pair_of_slots(pair, _):
        whole = 2 * pair + 1 < live
        slot = (2 * pair, jnp.where(whole, 2 * pair + 1, 2 * pair))
        weight = (None, jnp.where(whole, 1.0, 0.0).astype(F32))
        row = [info[s] for s in slot]
        col = [info[slots + s] for s in slot]
        left_shift = [lax.rem(LANES - c, LANES) for c in col]
        keep_left = [lane < LANES - c for c in col]
        keep_right = [lane >= c for c in col]

        for q in range(2):
            for at in range(0, win, CHUNK):
                for c in range(2):
                    parts = [
                        pltpu.roll(ext[c, t, pl.ds(row[q] + at, CHUNK), :], left_shift[q], 1) for t in range(3)
                    ]
                    for h in range(2):
                        owin[q, c, h, at : at + CHUNK, :] = jnp.where(keep_left[q], parts[h], parts[h + 1])

        for m in range(modes):
            for at in range(0, half, CHUNK):
                for h in range(2):
                    psi = ([], [])
                    for rows in (slice(at, at + CHUNK), slice(half + at, half + at + CHUNK)):
                        p_re = probe[0, m, rows, sides[h]]
                        p_im = probe[1, m, rows, sides[h]]
                        for q in range(2):
                            o_re = owin[q, 0, h, rows, :]
                            o_im = owin[q, 1, h, rows, :]
                            psi[q].append((p_re * o_re - p_im * o_im, p_re * o_im + p_im * o_re))
                    for q in range(2):
                        for c in range(2):
                            rows = slice(c * half + at, c * half + at + CHUNK)
                            xs[q, m, 0, rows, sides[h]] = (psi[q][0][c] + psi[q][1][c]).astype(BF16)
                            xs[q, m, 1, rows, sides[h]] = (psi[q][0][c] - psi[q][1][c]).astype(BF16)
            for q in range(2):
                for rp in range(2):
                    v = jnp.dot(fwd[rp], xs[q, m, rp], preferred_element_type=F32)
                    v = (
                        (v[:, :half] + v[:, half:]).astype(BF16),
                        (v[:, :half] - v[:, half:]).astype(BF16),
                    )
                    for pc in range(2):
                        for at in range(0, half, BLOCK):
                            for c in range(2):
                                hb[
                                    q, pc, (rp * half + at) // BLOCK, m * BLOCK : (m + 1) * BLOCK, sides[c]
                                ] = v[pc][c * half + at : c * half + at + BLOCK]

        for rb in range(blocks):
            for pc in range(2):
                for q in range(2):
                    field = jnp.dot(hb[q, pc, rb], bwd[pc], preferred_element_type=F32)
                    for at in range(0, BLOCK, CHUNK):
                        part = [field[m * BLOCK + at : m * BLOCK + at + CHUNK] for m in range(modes)]
                        total = 1.0
                        for f in part:
                            total = total + (f[:, :half] * f[:, :half] + f[:, half:] * f[:, half:])
                        f_row = rb * BLOCK + at
                        factor = 1.0 - meas[slot[q], f_row : f_row + CHUNK, sides[pc]].astype(F32) * lax.rsqrt(total)
                        if q == 1:
                            factor = factor * weight[q]
                        rp, f_row = divmod(f_row, half)
                        for m in range(modes):
                            for c in range(2):
                                gb[q, m, rp, c * half + f_row : c * half + f_row + CHUNK, sides[pc]] = (
                                    part[m][:, sides[c]] * factor
                                ).astype(BF16)

        for m in range(modes):
            for q in range(2):
                v0 = jnp.dot(bwd[0], gb[q, m, 0], preferred_element_type=F32)
                v1 = jnp.dot(bwd[1], gb[q, m, 1], preferred_element_type=F32)
                for side, v in enumerate(((v0 + v1).astype(BF16), (v0 - v1).astype(BF16))):
                    for at in range(0, half, BLOCK):
                        for pc in range(2):
                            for c in range(2):
                                kb[
                                    q, pc, (side * half + at) // BLOCK, m * BLOCK : (m + 1) * BLOCK, sides[c]
                                ] = v[c * half + at : c * half + at + BLOCK, sides[pc]]

        for rb in range(blocks):
            w = [
                [jnp.dot(kb[q, pc, rb], fwd[pc], preferred_element_type=F32) for pc in range(2)]
                for q in range(2)
            ]
            for at in range(0, BLOCK, CHUNK):
                rows = slice(rb * BLOCK + at, rb * BLOCK + at + CHUNK)
                g = [[[None, None], [None, None]] for q in range(2)]
                for h in range(2):
                    o = [[owin[q, c, h, rows, :] for c in range(2)] for q in range(2)]
                    for m in range(modes):
                        p_re = probe[0, m, rows, sides[h]]
                        p_im = probe[1, m, rows, sides[h]]
                        terms = []
                        for q in range(2):
                            w0, w1 = (v[m * BLOCK + at : m * BLOCK + at + CHUNK] for v in w[q])
                            chi = w0 + w1 if h == 0 else w0 - w1
                            c_re = chi[:, :half]
                            c_im = chi[:, half:]
                            t_re = p_re * c_re + p_im * c_im
                            t_im = p_re * c_im - p_im * c_re
                            g[q][0][h] = t_re if m == 0 else g[q][0][h] + t_re
                            g[q][1][h] = t_im if m == 0 else g[q][1][h] + t_im
                            o_re, o_im = o[q]
                            terms.append((o_re * c_re + o_im * c_im, o_re * c_im - o_im * c_re))
                        for c in range(2):
                            acc[c, m, rows, sides[h]] += terms[0][c] + terms[1][c]
                for q in range(2):
                    for c in range(2):
                        left = pltpu.roll(g[q][c][0], col[q], 1)
                        right = pltpu.roll(g[q][c][1], col[q], 1)
                        zero = jnp.zeros_like(left)
                        spread = (
                            jnp.where(keep_right[q], left, zero),
                            jnp.where(keep_right[q], right, left),
                            jnp.where(keep_right[q], zero, right),
                        )
                        for t in range(3):
                            sums[t][c, pl.ds(row[q] + rows.start, CHUNK), :] += spread[t]
        return 0

    lax.fori_loop(0, lax.div(live + 1, 2), pair_of_slots, 0)

    g_next[...] = mid[:, :tile_rows, :].astype(BF16)
    g_next_low[...] = mid[:, tile_rows:, :].astype(BF16)
    for m in range(modes):
        for at in range(0, win, 8):
            for h in range(2):
                to = (m * win + at) * 2 + 8 * h
                acc_keep[to : to + 8, :] = acc[core, m, at : at + 8, h * LANES : (h + 1) * LANES]
            pair = acc[1 - core, m, at : at + 8, :]
            to = (m * win + at) * 2
            acc_send[to : to + 16, :] = jnp.concatenate([pair[:, :LANES], pair[:, LANES:]], axis=0).astype(BF16)


def prepare_kernel(fwd, bwd, perm, probe, meas, fwd_out, bwd_out, probe_out, meas_out, swaps, raw, sems):
    copies = [
        pltpu.make_async_copy(source, target, sems.at[i])
        for i, (source, target) in enumerate(
            ((perm, swaps), (meas.at[0], raw), (probe, probe_out), (fwd, fwd_out), (bwd, bwd_out))
        )
    ]
    for copy in copies:
        copy.start()
    copies[0].wait()
    copies[1].wait()
    for s in range(raw.shape[0]):
        rows_done = jnp.dot(swaps[0], raw[s], preferred_element_type=F32).astype(BF16)
        meas_out[s] = jnp.dot(rows_done, swaps[1], preferred_element_type=F32).astype(BF16)
    for copy in copies[2:]:
        copy.wait()


def prepare(probe, measured):
    slots, win = measured.shape[1:3]
    fwd, bwd, perm = dft_tables(win)
    return pl.pallas_call(
        prepare_kernel,
        in_specs=[pl.BlockSpec(memory_space=pltpu.HBM)] * 5,
        out_specs=[pl.BlockSpec(memory_space=pltpu.VMEM)] * 4,
        out_shape=[
            jax.ShapeDtypeStruct(fwd.shape, BF16),
            jax.ShapeDtypeStruct(bwd.shape, BF16),
            jax.ShapeDtypeStruct(probe.shape, F32),
            jax.ShapeDtypeStruct(measured.shape[1:], BF16),
        ],
        scratch_shapes=[
            pltpu.VMEM(perm.shape, BF16),
            pltpu.VMEM(measured.shape[1:], BF16),
            pltpu.SemaphoreType.DMA((5,)),
        ],
        cost_estimate=pl.CostEstimate(flops=4 * slots * win**3, bytes_accessed=8 << 20, transcendentals=0),
        compiler_params=pltpu.CompilerParams(vmem_limit_bytes=8 * 1024 * 1024),
        name="prepare",
    )(jnp.asarray(fwd), jnp.asarray(bwd), jnp.asarray(perm), probe, measured)


def run_slots(info, fwd, bwd, probe, measured, own, own_low, nxt, nxt_low, sec, sec_low):
    tile_rows, tile_cols = own.shape[1:]
    modes, win = probe.shape[1:3]
    tall = (2, tile_rows + win, tile_cols)
    flat = (2 * modes * win, LANES)
    blocks = (2, win // BLOCK, modes * BLOCK, win)
    vmem = pl.BlockSpec(memory_space=pltpu.VMEM)
    return pl.pallas_call(
        slots_kernel,
        in_specs=[pl.BlockSpec(memory_space=pltpu.SMEM)] + [vmem] * 10,
        out_specs=[vmem] * 6,
        out_shape=[
            jax.ShapeDtypeStruct(tall, F32),
            jax.ShapeDtypeStruct(own.shape, BF16),
            jax.ShapeDtypeStruct(own_low.shape, BF16),
            jax.ShapeDtypeStruct(tall, F32),
            jax.ShapeDtypeStruct(flat, F32),
            jax.ShapeDtypeStruct(flat, BF16),
        ],
        scratch_shapes=[
            pltpu.VMEM((2, 3) + tall[1:], F32),
            pltpu.VMEM(tall, F32),
            pltpu.VMEM((2, modes, win, win), F32),
            pltpu.VMEM((2, 2, 2, win, LANES), F32),
            pltpu.VMEM((2, modes, 2, win, win), BF16),
            pltpu.VMEM((2,) + blocks, BF16),
            pltpu.VMEM((2, modes, 2, win, win), BF16),
            pltpu.VMEM((2,) + blocks, BF16),
        ],
        compiler_params=pltpu.CompilerParams(vmem_limit_bytes=22 * 1024 * 1024),
        name="slots",
    )(info, fwd, bwd, probe, measured, own, own_low, nxt, nxt_low, sec, sec_low)


def moved(value, target):
    n_rows = lax.axis_size("rows")
    n_cols = lax.axis_size("cols")
    pairs = []
    for a in range(n_rows):
        for b in range(n_cols):
            to_a, to_b = target(a, b)
            if 0 <= to_a < n_rows and 0 <= to_b < n_cols:
                pairs.append((a * n_cols + b, to_a * n_cols + to_b))
    return lax.ppermute(value, ("rows", "cols"), pairs)


def swap_cores(value):
    return moved(value, lambda a, b: (a, b ^ 1))


def local(object_field, probe_mode_stack, measured, corner_row, corner_col, count):
    tile_rows, tile_cols = object_field.shape[1:]
    modes, win = probe_mode_stack.shape[1:3]
    slot_count = measured.shape[1]
    devices = lax.axis_size("rows") * lax.axis_size("cols")
    col_at = lax.axis_index("cols")
    core = lax.rem(col_at, 2)

    top = object_field[:, :win, :]
    sec = moved(object_field, lambda a, b: (a, b - 2))
    sec_low = moved(top, lambda a, b: (a - 1, b - 2))
    own_low = moved(top, lambda a, b: (a - 1, b))
    prepared, sec = lax.optimization_barrier((prepare(probe_mode_stack, measured), sec))
    nxt_low = swap_cores(jnp.where(core == 0, sec_low, own_low))
    nxt = swap_cores(jnp.where(core == 0, sec, object_field))
    info = jnp.concatenate(
        [
            corner_row[0] - lax.axis_index("rows") * tile_rows,
            corner_col[0] - col_at * tile_cols,
            count[0],
            core[None],
        ]
    )
    g_own, g_next, g_next_low, g_sec, acc_keep, acc_send = run_slots(
        info, *prepared, object_field, own_low, nxt, nxt_low, sec, sec_low
    )

    acc_got = swap_cores(acc_send)
    near = swap_cores(g_next)
    chip_sum = (acc_keep + acc_got.astype(F32)).astype(BF16)
    chip_sum, near, near_low = lax.optimization_barrier((chip_sum, near, g_next_low))
    near = jnp.concatenate([near, swap_cores(near_low)], axis=1).astype(F32)
    none = jnp.zeros_like(near)
    outward = (g_sec + jnp.where(core == 0, near, none)).astype(BF16)
    far = moved(outward, lambda a, b: (a, b + 2))
    total = g_own + jnp.where(core == 1, near, none) + far.astype(F32)
    rim = moved(total[:, tile_rows:].astype(BF16), lambda a, b: (a + 1, b))

    groups = [[i for i in range(devices) if i % 2 == c] for c in range(2)]
    exchange = functools.partial(
        lax.all_to_all, axis_name=("rows", "cols"), split_axis=0, concat_axis=0,
        axis_index_groups=groups, tiled=True,
    )
    share = exchange(chip_sum.reshape(devices // 2, -1, LANES))
    scale = 1.0 / jnp.sqrt(jnp.float32(devices * slot_count))
    share = (jnp.sum(share.astype(F32), axis=0) * scale).astype(BF16)
    mine = exchange(jnp.broadcast_to(share[None], (devices // 2,) + share.shape))
    mine, rim = lax.optimization_barrier((mine, rim))
    mine = mine.reshape(-1, LANES)
    part = lax.broadcasted_iota(jnp.int32, (2,) + mine.shape, 0)
    probe_grad = jnp.where(part == core, mine[None], swap_cores(mine)[None]).astype(F32)
    probe_grad = probe_grad.reshape(2, modes, win // 8, 2, 8, LANES).transpose(0, 1, 2, 4, 3, 5)
    probe_grad = probe_grad.reshape(2, modes, win, win)

    object_grad = total[:, :tile_rows] + jnp.pad(rim.astype(F32), ((0, 0), (0, tile_rows - win), (0, 0)))
    return (object_grad, probe_grad)


def solution(mesh):
    placed = (
        P(None, "rows", "cols"),
        P(),
        P("rows", "cols", None, None),
        P("rows", "cols"),
        P("rows", "cols"),
        P("rows", "cols"),
    )
    return jax.shard_map(
        local, mesh=mesh, in_specs=placed, out_specs=(P(None, "rows", "cols"), P()), check_vma=False
    )
```

```python
import functools

import jax
import jax.numpy as jnp
import ml_dtypes
import numpy as np
from jax import lax
from jax.experimental import pallas as pl
from jax.experimental.pallas import tpu as pltpu
from jax.sharding import PartitionSpec as P

F32 = jnp.float32
BF16 = jnp.bfloat16
LANES = 128
CHUNK = 16
BLOCK = 64


def dft_tables(win):
    half = win // 2
    k = np.arange(win)[:, None]
    j = np.arange(win)[None, :]
    angle = (k * j % win).astype(np.float64) * (2.0 * np.pi / win)
    re = np.cos(angle) / np.sqrt(win)
    im = -np.sin(angle) / np.sqrt(win)
    tables = []
    for parity in range(2):
        cr = re[parity::2, :half]
        ci = im[parity::2, :half]
        tables.append(np.block([[cr, -ci], [ci, cr]]))
    forward = np.stack(tables)
    backward = np.stack([t.T for t in tables])
    order = np.concatenate([np.arange(0, win, 2), np.arange(1, win, 2)])
    permute = np.zeros((win, win))
    permute[np.arange(win), order] = 1.0
    both = np.stack([permute, permute.T])
    cast = lambda a: a.astype(ml_dtypes.bfloat16)
    return cast(forward), cast(backward), cast(both)


def slots_kernel(
    info, fwd, bwd, probe, meas, own, own_low, nxt, nxt_low, sec, sec_low,
    g_own, g_next, g_next_low, g_sec, acc_keep, acc_send,
    ext, mid, acc, owin, xs, hb, gb, kb,
):
    slots = meas.shape[0]
    live = info[2 * slots]
    core = info[2 * slots + 1]
    modes = probe.shape[1]
    win = probe.shape[2]
    half = win // 2
    blocks = win // BLOCK
    tile_rows = own.shape[1]
    sums = (g_own, mid, g_sec)

    for c in range(2):
        for t, (top, bottom) in enumerate(((own, own_low), (nxt, nxt_low), (sec, sec_low))):
            ext[c, t, :tile_rows, :] = top[c].astype(F32)
            ext[c, t, tile_rows:, :] = bottom[c].astype(F32)
    for ref in sums + (acc,):
        ref[...] = jnp.zeros_like(ref)

    sides = (slice(0, LANES), slice(LANES, 2 * LANES))
    lane = lax.broadcasted_iota(jnp.int32, (CHUNK, LANES), 1)

    def pair_of_slots(pair, _):
        whole = 2 * pair + 1 < live
        slot = (2 * pair, jnp.where(whole, 2 * pair + 1, 2 * pair))
        weight = (None, jnp.where(whole, 1.0, 0.0).astype(F32))
        row = [info[s] for s in slot]
        col = [info[slots + s] for s in slot]
        left_shift = [lax.rem(LANES - c, LANES) for c in col]
        keep_left = [lane < LANES - c for c in col]
        keep_right = [lane >= c for c in col]

        for q in range(2):
            for at in range(0, win, CHUNK):
                for c in range(2):
                    parts = [
                        pltpu.roll(ext[c, t, pl.ds(row[q] + at, CHUNK), :], left_shift[q], 1) for t in range(3)
                    ]
                    for h in range(2):
                        owin[q, c, h, at : at + CHUNK, :] = jnp.where(keep_left[q], parts[h], parts[h + 1])

        for m in range(modes):
            for at in range(0, half, CHUNK):
                for h in range(2):
                    psi = ([], [])
                    for rows in (slice(at, at + CHUNK), slice(half + at, half + at + CHUNK)):
                        p_re = probe[0, m, rows, sides[h]]
                        p_im = probe[1, m, rows, sides[h]]
                        for q in range(2):
                            o_re = owin[q, 0, h, rows, :]
                            o_im = owin[q, 1, h, rows, :]
                            psi[q].append((p_re * o_re - p_im * o_im, p_re * o_im + p_im * o_re))
                    for q in range(2):
                        for c in range(2):
                            rows = slice(c * half + at, c * half + at + CHUNK)
                            xs[q, m, 0, rows, sides[h]] = (psi[q][0][c] + psi[q][1][c]).astype(BF16)
                            xs[q, m, 1, rows, sides[h]] = (psi[q][0][c] - psi[q][1][c]).astype(BF16)
            for q in range(2):
                for rp in range(2):
                    v = jnp.dot(fwd[rp], xs[q, m, rp], preferred_element_type=F32)
                    v = (
                        (v[:, :half] + v[:, half:]).astype(BF16),
                        (v[:, :half] - v[:, half:]).astype(BF16),
                    )
                    for pc in range(2):
                        for at in range(0, half, BLOCK):
                            for c in range(2):
                                hb[
                                    q, pc, (rp * half + at) // BLOCK, m * BLOCK : (m + 1) * BLOCK, sides[c]
                                ] = v[pc][c * half + at : c * half + at + BLOCK]

        for rb in range(blocks):
            for pc in range(2):
                for q in range(2):
                    field = jnp.dot(hb[q, pc, rb], bwd[pc], preferred_element_type=F32)
                    for at in range(0, BLOCK, CHUNK):
                        part = [field[m * BLOCK + at : m * BLOCK + at + CHUNK] for m in range(modes)]
                        total = 1.0
                        for f in part:
                            total = total + (f[:, :half] * f[:, :half] + f[:, half:] * f[:, half:])
                        f_row = rb * BLOCK + at
                        factor = 1.0 - meas[slot[q], f_row : f_row + CHUNK, sides[pc]].astype(F32) * lax.rsqrt(total)
                        if q == 1:
                            factor = factor * weight[q]
                        rp, f_row = divmod(f_row, half)
                        for m in range(modes):
                            for c in range(2):
                                gb[q, m, rp, c * half + f_row : c * half + f_row + CHUNK, sides[pc]] = (
                                    part[m][:, sides[c]] * factor
                                ).astype(BF16)

        for m in range(modes):
            for q in range(2):
                v0 = jnp.dot(bwd[0], gb[q, m, 0], preferred_element_type=F32)
                v1 = jnp.dot(bwd[1], gb[q, m, 1], preferred_element_type=F32)
                for side, v in enumerate(((v0 + v1).astype(BF16), (v0 - v1).astype(BF16))):
                    for at in range(0, half, BLOCK):
                        for pc in range(2):
                            for c in range(2):
                                kb[
                                    q, pc, (side * half + at) // BLOCK, m * BLOCK : (m + 1) * BLOCK, sides[c]
                                ] = v[c * half + at : c * half + at + BLOCK, sides[pc]]

        for rb in range(blocks):
            w = [
                [jnp.dot(kb[q, pc, rb], fwd[pc], preferred_element_type=F32) for pc in range(2)]
                for q in range(2)
            ]
            for at in range(0, BLOCK, CHUNK):
                rows = slice(rb * BLOCK + at, rb * BLOCK + at + CHUNK)
                g = [[[None, None], [None, None]] for q in range(2)]
                for h in range(2):
                    o = [[owin[q, c, h, rows, :] for c in range(2)] for q in range(2)]
                    for m in range(modes):
                        p_re = probe[0, m, rows, sides[h]]
                        p_im = probe[1, m, rows, sides[h]]
                        terms = []
                        for q in range(2):
                            w0, w1 = (v[m * BLOCK + at : m * BLOCK + at + CHUNK] for v in w[q])
                            chi = w0 + w1 if h == 0 else w0 - w1
                            c_re = chi[:, :half]
                            c_im = chi[:, half:]
                            t_re = p_re * c_re + p_im * c_im
                            t_im = p_re * c_im - p_im * c_re
                            g[q][0][h] = t_re if m == 0 else g[q][0][h] + t_re
                            g[q][1][h] = t_im if m == 0 else g[q][1][h] + t_im
                            o_re, o_im = o[q]
                            terms.append((o_re * c_re + o_im * c_im, o_re * c_im - o_im * c_re))
                        for c in range(2):
                            acc[c, m, rows, sides[h]] += terms[0][c] + terms[1][c]
                for q in range(2):
                    for c in range(2):
                        left = pltpu.roll(g[q][c][0], col[q], 1)
                        right = pltpu.roll(g[q][c][1], col[q], 1)
                        zero = jnp.zeros_like(left)
                        spread = (
                            jnp.where(keep_right[q], left, zero),
                            jnp.where(keep_right[q], right, left),
                            jnp.where(keep_right[q], zero, right),
                        )
                        for t in range(3):
                            sums[t][c, pl.ds(row[q] + rows.start, CHUNK), :] += spread[t]
        return 0

    lax.fori_loop(0, lax.div(live + 1, 2), pair_of_slots, 0)

    g_next[...] = mid[:, :tile_rows, :].astype(BF16)
    g_next_low[...] = mid[:, tile_rows:, :].astype(BF16)
    for m in range(modes):
        for at in range(0, win, 8):
            for h in range(2):
                to = (m * win + at) * 2 + 8 * h
                acc_keep[to : to + 8, :] = acc[core, m, at : at + 8, h * LANES : (h + 1) * LANES]
            pair = acc[1 - core, m, at : at + 8, :]
            to = (m * win + at) * 2
            acc_send[to : to + 16, :] = jnp.concatenate([pair[:, :LANES], pair[:, LANES:]], axis=0).astype(BF16)


def prepare_kernel(fwd, bwd, perm, probe, meas, fwd_out, bwd_out, probe_out, meas_out, swaps, raw, sems):
    copies = [
        pltpu.make_async_copy(source, target, sems.at[i])
        for i, (source, target) in enumerate(
            ((perm, swaps), (meas.at[0], raw), (probe, probe_out), (fwd, fwd_out), (bwd, bwd_out))
        )
    ]
    for copy in copies:
        copy.start()
    copies[0].wait()
    copies[1].wait()
    for s in range(raw.shape[0]):
        rows_done = jnp.dot(swaps[0], raw[s], preferred_element_type=F32).astype(BF16)
        meas_out[s] = jnp.dot(rows_done, swaps[1], preferred_element_type=F32).astype(BF16)
    for copy in copies[2:]:
        copy.wait()


def prepare(probe, measured):
    slots, win = measured.shape[1:3]
    fwd, bwd, perm = dft_tables(win)
    return pl.pallas_call(
        prepare_kernel,
        in_specs=[pl.BlockSpec(memory_space=pltpu.HBM)] * 5,
        out_specs=[pl.BlockSpec(memory_space=pltpu.VMEM)] * 4,
        out_shape=[
            jax.ShapeDtypeStruct(fwd.shape, BF16),
            jax.ShapeDtypeStruct(bwd.shape, BF16),
            jax.ShapeDtypeStruct(probe.shape, F32),
            jax.ShapeDtypeStruct(measured.shape[1:], BF16),
        ],
        scratch_shapes=[
            pltpu.VMEM(perm.shape, BF16),
            pltpu.VMEM(measured.shape[1:], BF16),
            pltpu.SemaphoreType.DMA((5,)),
        ],
        cost_estimate=pl.CostEstimate(flops=4 * slots * win**3, bytes_accessed=8 << 20, transcendentals=0),
        compiler_params=pltpu.CompilerParams(vmem_limit_bytes=8 * 1024 * 1024),
        name="prepare",
    )(jnp.asarray(fwd), jnp.asarray(bwd), jnp.asarray(perm), probe, measured)


def run_slots(info, fwd, bwd, probe, measured, own, own_low, nxt, nxt_low, sec, sec_low):
    tile_rows, tile_cols = own.shape[1:]
    modes, win = probe.shape[1:3]
    tall = (2, tile_rows + win, tile_cols)
    flat = (2 * modes * win, LANES)
    blocks = (2, win // BLOCK, modes * BLOCK, win)
    vmem = pl.BlockSpec(memory_space=pltpu.VMEM)
    return pl.pallas_call(
        slots_kernel,
        in_specs=[pl.BlockSpec(memory_space=pltpu.SMEM)] + [vmem] * 10,
        out_specs=[vmem] * 6,
        out_shape=[
            jax.ShapeDtypeStruct(tall, F32),
            jax.ShapeDtypeStruct(own.shape, BF16),
            jax.ShapeDtypeStruct(own_low.shape, BF16),
            jax.ShapeDtypeStruct(tall, F32),
            jax.ShapeDtypeStruct(flat, F32),
            jax.ShapeDtypeStruct(flat, BF16),
        ],
        scratch_shapes=[
            pltpu.VMEM((2, 3) + tall[1:], F32),
            pltpu.VMEM(tall, F32),
            pltpu.VMEM((2, modes, win, win), F32),
            pltpu.VMEM((2, 2, 2, win, LANES), F32),
            pltpu.VMEM((2, modes, 2, win, win), BF16),
            pltpu.VMEM((2,) + blocks, BF16),
            pltpu.VMEM((2, modes, 2, win, win), BF16),
            pltpu.VMEM((2,) + blocks, BF16),
        ],
        compiler_params=pltpu.CompilerParams(vmem_limit_bytes=22 * 1024 * 1024),
        name="slots",
    )(info, fwd, bwd, probe, measured, own, own_low, nxt, nxt_low, sec, sec_low)


def moved(value, target):
    n_rows = lax.axis_size("rows")
    n_cols = lax.axis_size("cols")
    pairs = []
    for a in range(n_rows):
        for b in range(n_cols):
            to_a, to_b = target(a, b)
            if 0 <= to_a < n_rows and 0 <= to_b < n_cols:
                pairs.append((a * n_cols + b, to_a * n_cols + to_b))
    return lax.ppermute(value, ("rows", "cols"), pairs)


def swap_cores(value):
    return moved(value, lambda a, b: (a, b ^ 1))


def local(object_field, probe_mode_stack, measured, corner_row, corner_col, count):
    tile_rows, tile_cols = object_field.shape[1:]
    modes, win = probe_mode_stack.shape[1:3]
    slot_count = measured.shape[1]
    devices = lax.axis_size("rows") * lax.axis_size("cols")
    col_at = lax.axis_index("cols")
    core = lax.rem(col_at, 2)

    top = object_field[:, :win, :]
    sec = moved(object_field, lambda a, b: (a, b - 2))
    sec_low = moved(top, lambda a, b: (a - 1, b - 2))
    own_low = moved(top, lambda a, b: (a - 1, b))
    prepared, sec = lax.optimization_barrier((prepare(probe_mode_stack, measured), sec))
    nxt_low = swap_cores(jnp.where(core == 0, sec_low, own_low))
    nxt = swap_cores(jnp.where(core == 0, sec, object_field))
    info = jnp.concatenate(
        [
            corner_row[0] - lax.axis_index("rows") * tile_rows,
            corner_col[0] - col_at * tile_cols,
            count[0],
            core[None],
        ]
    )
    g_own, g_next, g_next_low, g_sec, acc_keep, acc_send = run_slots(
        info, *prepared, object_field, own_low, nxt, nxt_low, sec, sec_low
    )

    acc_got = swap_cores(acc_send)
    near = swap_cores(g_next)
    chip_sum = (acc_keep + acc_got.astype(F32)).astype(BF16)
    chip_sum, near, near_low = lax.optimization_barrier((chip_sum, near, g_next_low))
    near = jnp.concatenate([near, swap_cores(near_low)], axis=1).astype(F32)
    none = jnp.zeros_like(near)
    outward = (g_sec + jnp.where(core == 0, near, none)).astype(BF16)
    far = moved(outward, lambda a, b: (a, b + 2))
    inner = jnp.where(core == 1, near, none)
    below = g_own[:, tile_rows:] + inner[:, tile_rows:] + far[:, tile_rows:].astype(F32)
    rim = moved(below.astype(BF16), lambda a, b: (a + 1, b))

    groups = [[i for i in range(devices) if i % 2 == c] for c in range(2)]
    exchange = functools.partial(
        lax.all_to_all, axis_name=("rows", "cols"), split_axis=0, concat_axis=0,
        axis_index_groups=groups, tiled=True,
    )
    share = exchange(chip_sum.reshape(devices // 2, -1, LANES))
    scale = 1.0 / jnp.sqrt(jnp.float32(devices * slot_count))
    share = (jnp.sum(share.astype(F32), axis=0) * scale).astype(BF16)
    mine = exchange(jnp.broadcast_to(share[None], (devices // 2,) + share.shape))
    mine, rim = lax.optimization_barrier((mine, rim))
    mine = mine.reshape(-1, LANES)
    part = lax.broadcasted_iota(jnp.int32, (2,) + mine.shape, 0)
    probe_grad = jnp.where(part == core, mine[None], swap_cores(mine)[None]).astype(F32)
    probe_grad = probe_grad.reshape(2, modes, win // 8, 2, 8, LANES).transpose(0, 1, 2, 4, 3, 5)
    probe_grad = probe_grad.reshape(2, modes, win, win)

    rim = jnp.pad(rim.astype(F32), ((0, 0), (0, tile_rows - win), (0, 0)))
    object_grad = g_own[:, :tile_rows] + inner[:, :tile_rows] + far[:, :tile_rows].astype(F32) + rim
    return (object_grad, probe_grad)


def solution(mesh):
    placed = (
        P(None, "rows", "cols"),
        P(),
        P("rows", "cols", None, None),
        P("rows", "cols"),
        P("rows", "cols"),
        P("rows", "cols"),
    )
    return jax.shard_map(
        local, mesh=mesh, in_specs=placed, out_specs=(P(None, "rows", "cols"), P()), check_vma=False
    )
```

```python
import functools

import jax
import jax.numpy as jnp
import ml_dtypes
import numpy as np
from jax import lax
from jax.experimental import pallas as pl
from jax.experimental.pallas import tpu as pltpu
from jax.sharding import PartitionSpec as P

F32 = jnp.float32
BF16 = jnp.bfloat16
LANES = 128
CHUNK = 16
BLOCK = 64


def dft_tables(win):
    half = win // 2
    k = np.arange(win)[:, None]
    j = np.arange(win)[None, :]
    angle = (k * j % win).astype(np.float64) * (2.0 * np.pi / win)
    re = np.cos(angle) / np.sqrt(win)
    im = -np.sin(angle) / np.sqrt(win)
    tables = []
    for parity in range(2):
        cr = re[parity::2, :half]
        ci = im[parity::2, :half]
        tables.append(np.block([[cr, -ci], [ci, cr]]))
    forward = np.stack(tables)
    backward = np.stack([t.T for t in tables])
    order = np.concatenate([np.arange(0, win, 2), np.arange(1, win, 2)])
    permute = np.zeros((win, win))
    permute[np.arange(win), order] = 1.0
    both = np.stack([permute, permute.T])
    cast = lambda a: a.astype(ml_dtypes.bfloat16)
    return cast(forward), cast(backward), cast(both)


def slots_kernel(
    info, fwd, bwd, probe, meas, own, own_low, nxt, nxt_low, sec, sec_low,
    g_own, g_next, g_next_low, g_sec, acc_keep, acc_send,
    ext, mid, acc, owin, xs, hb, gb, kb,
):
    slots = meas.shape[0]
    live = info[2 * slots]
    core = info[2 * slots + 1]
    modes = probe.shape[1]
    win = probe.shape[2]
    half = win // 2
    blocks = win // BLOCK
    tile_rows = own.shape[1]
    sums = (g_own, mid, g_sec)

    for c in range(2):
        for t, (top, bottom) in enumerate(((own, own_low), (nxt, nxt_low), (sec, sec_low))):
            ext[c, t, :tile_rows, :] = top[c].astype(F32)
            ext[c, t, tile_rows:, :] = bottom[c].astype(F32)
    for ref in sums + (acc,):
        ref[...] = jnp.zeros_like(ref)

    sides = (slice(0, LANES), slice(LANES, 2 * LANES))
    lane = lax.broadcasted_iota(jnp.int32, (CHUNK, LANES), 1)

    def pair_of_slots(pair, _):
        whole = 2 * pair + 1 < live
        slot = (2 * pair, jnp.where(whole, 2 * pair + 1, 2 * pair))
        weight = (None, jnp.where(whole, 1.0, 0.0).astype(F32))
        row = [info[s] for s in slot]
        col = [info[slots + s] for s in slot]
        left_shift = [lax.rem(LANES - c, LANES) for c in col]
        keep_left = [lane < LANES - c for c in col]
        keep_right = [lane >= c for c in col]

        for q in range(2):
            for at in range(0, win, CHUNK):
                for c in range(2):
                    parts = [
                        pltpu.roll(ext[c, t, pl.ds(row[q] + at, CHUNK), :], left_shift[q], 1) for t in range(3)
                    ]
                    for h in range(2):
                        owin[q, c, h, at : at + CHUNK, :] = jnp.where(keep_left[q], parts[h], parts[h + 1])

        def exit_waves(m):
            for at in range(0, half, CHUNK):
                for h in range(2):
                    psi = ([], [])
                    for rows in (slice(at, at + CHUNK), slice(half + at, half + at + CHUNK)):
                        p_re = probe[0, m, rows, sides[h]]
                        p_im = probe[1, m, rows, sides[h]]
                        for q in range(2):
                            o_re = owin[q, 0, h, rows, :]
                            o_im = owin[q, 1, h, rows, :]
                            psi[q].append((p_re * o_re - p_im * o_im, p_re * o_im + p_im * o_re))
                    for q in range(2):
                        for c in range(2):
                            rows = slice(c * half + at, c * half + at + CHUNK)
                            xs[q, m, 0, rows, sides[h]] = (psi[q][0][c] + psi[q][1][c]).astype(BF16)
                            xs[q, m, 1, rows, sides[h]] = (psi[q][0][c] - psi[q][1][c]).astype(BF16)

        def half_products(job):
            m, q = job
            if q == 0:
                exit_waves(m)
            return [jnp.dot(fwd[rp], xs[q, m, rp], preferred_element_type=F32) for rp in range(2)]

        def keep_half_done(job, values):
            m, q = job
            for rp, v in enumerate(values):
                v = (
                    (v[:, :half] + v[:, half:]).astype(BF16),
                    (v[:, :half] - v[:, half:]).astype(BF16),
                )
                for pc in range(2):
                    for at in range(0, half, BLOCK):
                        for c in range(2):
                            hb[
                                q, pc, (rp * half + at) // BLOCK, m * BLOCK : (m + 1) * BLOCK, sides[c]
                            ] = v[pc][c * half + at : c * half + at + BLOCK]

        def far_products(job):
            rb, pc, q = job
            return jnp.dot(hb[q, pc, rb], bwd[pc], preferred_element_type=F32)

        def correct(job, field):
            rb, pc, q = job
            for at in range(0, BLOCK, CHUNK):
                part = [field[m * BLOCK + at : m * BLOCK + at + CHUNK] for m in range(modes)]
                total = 1.0
                for f in part:
                    total = total + (f[:, :half] * f[:, :half] + f[:, half:] * f[:, half:])
                f_row = rb * BLOCK + at
                factor = 1.0 - meas[slot[q], f_row : f_row + CHUNK, sides[pc]].astype(F32) * lax.rsqrt(total)
                if q == 1:
                    factor = factor * weight[q]
                rp, f_row = divmod(f_row, half)
                for m in range(modes):
                    for c in range(2):
                        gb[q, m, rp, c * half + f_row : c * half + f_row + CHUNK, sides[pc]] = (
                            part[m][:, sides[c]] * factor
                        ).astype(BF16)

        def back_products(job):
            m, q = job
            return [jnp.dot(bwd[rp], gb[q, m, rp], preferred_element_type=F32) for rp in range(2)]

        def keep_back_half(job, values):
            m, q = job
            v0, v1 = values
            for side, v in enumerate(((v0 + v1).astype(BF16), (v0 - v1).astype(BF16))):
                for at in range(0, half, BLOCK):
                    for pc in range(2):
                        for c in range(2):
                            kb[
                                q, pc, (side * half + at) // BLOCK, m * BLOCK : (m + 1) * BLOCK, sides[c]
                            ] = v[c * half + at : c * half + at + BLOCK, sides[pc]]

        def chi_products(rb):
            return [
                [jnp.dot(kb[q, pc, rb], fwd[pc], preferred_element_type=F32) for pc in range(2)]
                for q in range(2)
            ]

        def gather_up(rb, w):
            for at in range(0, BLOCK, CHUNK):
                rows = slice(rb * BLOCK + at, rb * BLOCK + at + CHUNK)
                g = [[[None, None], [None, None]] for q in range(2)]
                for h in range(2):
                    o = [[owin[q, c, h, rows, :] for c in range(2)] for q in range(2)]
                    for m in range(modes):
                        p_re = probe[0, m, rows, sides[h]]
                        p_im = probe[1, m, rows, sides[h]]
                        terms = []
                        for q in range(2):
                            w0, w1 = (v[m * BLOCK + at : m * BLOCK + at + CHUNK] for v in w[q])
                            chi = w0 + w1 if h == 0 else w0 - w1
                            c_re = chi[:, :half]
                            c_im = chi[:, half:]
                            t_re = p_re * c_re + p_im * c_im
                            t_im = p_re * c_im - p_im * c_re
                            g[q][0][h] = t_re if m == 0 else g[q][0][h] + t_re
                            g[q][1][h] = t_im if m == 0 else g[q][1][h] + t_im
                            o_re, o_im = o[q]
                            terms.append((o_re * c_re + o_im * c_im, o_re * c_im - o_im * c_re))
                        for c in range(2):
                            acc[c, m, rows, sides[h]] += terms[0][c] + terms[1][c]
                for q in range(2):
                    for c in range(2):
                        left = pltpu.roll(g[q][c][0], col[q], 1)
                        right = pltpu.roll(g[q][c][1], col[q], 1)
                        zero = jnp.zeros_like(left)
                        spread = (
                            jnp.where(keep_right[q], left, zero),
                            jnp.where(keep_right[q], right, left),
                            jnp.where(keep_right[q], zero, right),
                        )
                        for t in range(3):
                            sums[t][c, pl.ds(row[q] + rows.start, CHUNK), :] += spread[t]

        def one_ahead(jobs, products, use):
            ready = products(jobs[0])
            for n, job in enumerate(jobs):
                later = products(jobs[n + 1]) if n + 1 < len(jobs) else None
                use(job, ready)
                ready = later

        by_mode = [(m, q) for m in range(modes) for q in range(2)]
        one_ahead(by_mode, half_products, keep_half_done)
        one_ahead(
            [(rb, pc, q) for rb in range(blocks) for pc in range(2) for q in range(2)], far_products, correct
        )
        one_ahead(by_mode, back_products, keep_back_half)
        one_ahead(list(range(blocks)), chi_products, gather_up)
        return 0

    lax.fori_loop(0, lax.div(live + 1, 2), pair_of_slots, 0)

    g_next[...] = mid[:, :tile_rows, :].astype(BF16)
    g_next_low[...] = mid[:, tile_rows:, :].astype(BF16)
    for m in range(modes):
        for at in range(0, win, 8):
            for h in range(2):
                to = (m * win + at) * 2 + 8 * h
                acc_keep[to : to + 8, :] = acc[core, m, at : at + 8, h * LANES : (h + 1) * LANES]
            pair = acc[1 - core, m, at : at + 8, :]
            to = (m * win + at) * 2
            acc_send[to : to + 16, :] = jnp.concatenate([pair[:, :LANES], pair[:, LANES:]], axis=0).astype(BF16)


def prepare_kernel(fwd, bwd, perm, probe, meas, fwd_out, bwd_out, probe_out, meas_out, swaps, raw, sems):
    copies = [
        pltpu.make_async_copy(source, target, sems.at[i])
        for i, (source, target) in enumerate(
            ((perm, swaps), (meas.at[0], raw), (probe, probe_out), (fwd, fwd_out), (bwd, bwd_out))
        )
    ]
    for copy in copies:
        copy.start()
    copies[0].wait()
    copies[1].wait()
    for s in range(raw.shape[0]):
        rows_done = jnp.dot(swaps[0], raw[s], preferred_element_type=F32).astype(BF16)
        meas_out[s] = jnp.dot(rows_done, swaps[1], preferred_element_type=F32).astype(BF16)
    for copy in copies[2:]:
        copy.wait()


def prepare(probe, measured):
    slots, win = measured.shape[1:3]
    fwd, bwd, perm = dft_tables(win)
    return pl.pallas_call(
        prepare_kernel,
        in_specs=[pl.BlockSpec(memory_space=pltpu.HBM)] * 5,
        out_specs=[pl.BlockSpec(memory_space=pltpu.VMEM)] * 4,
        out_shape=[
            jax.ShapeDtypeStruct(fwd.shape, BF16),
            jax.ShapeDtypeStruct(bwd.shape, BF16),
            jax.ShapeDtypeStruct(probe.shape, F32),
            jax.ShapeDtypeStruct(measured.shape[1:], BF16),
        ],
        scratch_shapes=[
            pltpu.VMEM(perm.shape, BF16),
            pltpu.VMEM(measured.shape[1:], BF16),
            pltpu.SemaphoreType.DMA((5,)),
        ],
        cost_estimate=pl.CostEstimate(flops=4 * slots * win**3, bytes_accessed=8 << 20, transcendentals=0),
        compiler_params=pltpu.CompilerParams(vmem_limit_bytes=8 * 1024 * 1024),
        name="prepare",
    )(jnp.asarray(fwd), jnp.asarray(bwd), jnp.asarray(perm), probe, measured)


def run_slots(info, fwd, bwd, probe, measured, own, own_low, nxt, nxt_low, sec, sec_low):
    tile_rows, tile_cols = own.shape[1:]
    modes, win = probe.shape[1:3]
    tall = (2, tile_rows + win, tile_cols)
    flat = (2 * modes * win, LANES)
    blocks = (2, win // BLOCK, modes * BLOCK, win)
    vmem = pl.BlockSpec(memory_space=pltpu.VMEM)
    return pl.pallas_call(
        slots_kernel,
        in_specs=[pl.BlockSpec(memory_space=pltpu.SMEM)] + [vmem] * 10,
        out_specs=[vmem] * 6,
        out_shape=[
            jax.ShapeDtypeStruct(tall, F32),
            jax.ShapeDtypeStruct(own.shape, BF16),
            jax.ShapeDtypeStruct(own_low.shape, BF16),
            jax.ShapeDtypeStruct(tall, F32),
            jax.ShapeDtypeStruct(flat, F32),
            jax.ShapeDtypeStruct(flat, BF16),
        ],
        scratch_shapes=[
            pltpu.VMEM((2, 3) + tall[1:], F32),
            pltpu.VMEM(tall, F32),
            pltpu.VMEM((2, modes, win, win), F32),
            pltpu.VMEM((2, 2, 2, win, LANES), F32),
            pltpu.VMEM((2, modes, 2, win, win), BF16),
            pltpu.VMEM((2,) + blocks, BF16),
            pltpu.VMEM((2, modes, 2, win, win), BF16),
            pltpu.VMEM((2,) + blocks, BF16),
        ],
        compiler_params=pltpu.CompilerParams(vmem_limit_bytes=22 * 1024 * 1024),
        name="slots",
    )(info, fwd, bwd, probe, measured, own, own_low, nxt, nxt_low, sec, sec_low)


def moved(value, target):
    n_rows = lax.axis_size("rows")
    n_cols = lax.axis_size("cols")
    pairs = []
    for a in range(n_rows):
        for b in range(n_cols):
            to_a, to_b = target(a, b)
            if 0 <= to_a < n_rows and 0 <= to_b < n_cols:
                pairs.append((a * n_cols + b, to_a * n_cols + to_b))
    return lax.ppermute(value, ("rows", "cols"), pairs)


def swap_cores(value):
    return moved(value, lambda a, b: (a, b ^ 1))


def local(object_field, probe_mode_stack, measured, corner_row, corner_col, count):
    tile_rows, tile_cols = object_field.shape[1:]
    modes, win = probe_mode_stack.shape[1:3]
    slot_count = measured.shape[1]
    devices = lax.axis_size("rows") * lax.axis_size("cols")
    col_at = lax.axis_index("cols")
    core = lax.rem(col_at, 2)

    top = object_field[:, :win, :]
    sec = moved(object_field, lambda a, b: (a, b - 2))
    sec_low = moved(top, lambda a, b: (a - 1, b - 2))
    own_low = moved(top, lambda a, b: (a - 1, b))
    prepared, sec = lax.optimization_barrier((prepare(probe_mode_stack, measured), sec))
    nxt_low = swap_cores(jnp.where(core == 0, sec_low, own_low))
    nxt = swap_cores(jnp.where(core == 0, sec, object_field))
    info = jnp.concatenate(
        [
            corner_row[0] - lax.axis_index("rows") * tile_rows,
            corner_col[0] - col_at * tile_cols,
            count[0],
            core[None],
        ]
    )
    g_own, g_next, g_next_low, g_sec, acc_keep, acc_send = run_slots(
        info, *prepared, object_field, own_low, nxt, nxt_low, sec, sec_low
    )

    acc_got = swap_cores(acc_send)
    near = swap_cores(g_next)
    chip_sum = (acc_keep + acc_got.astype(F32)).astype(BF16)
    chip_sum, near, near_low = lax.optimization_barrier((chip_sum, near, g_next_low))
    near = jnp.concatenate([near, swap_cores(near_low)], axis=1).astype(F32)
    none = jnp.zeros_like(near)
    outward = (g_sec + jnp.where(core == 0, near, none)).astype(BF16)
    far = moved(outward, lambda a, b: (a, b + 2))
    total = g_own + jnp.where(core == 1, near, none) + far.astype(F32)
    rim = moved(total[:, tile_rows:].astype(BF16), lambda a, b: (a + 1, b))

    groups = [[i for i in range(devices) if i % 2 == c] for c in range(2)]
    exchange = functools.partial(
        lax.all_to_all, axis_name=("rows", "cols"), split_axis=0, concat_axis=0,
        axis_index_groups=groups, tiled=True,
    )
    share = exchange(chip_sum.reshape(devices // 2, -1, LANES))
    scale = 1.0 / jnp.sqrt(jnp.float32(devices * slot_count))
    share = (jnp.sum(share.astype(F32), axis=0) * scale).astype(BF16)
    mine = exchange(jnp.broadcast_to(share[None], (devices // 2,) + share.shape))
    mine, rim = lax.optimization_barrier((mine, rim))
    mine = mine.reshape(-1, LANES)
    part = lax.broadcasted_iota(jnp.int32, (2,) + mine.shape, 0)
    probe_grad = jnp.where(part == core, mine[None], swap_cores(mine)[None]).astype(F32)
    probe_grad = probe_grad.reshape(2, modes, win // 8, 2, 8, LANES).transpose(0, 1, 2, 4, 3, 5)
    probe_grad = probe_grad.reshape(2, modes, win, win)

    object_grad = total[:, :tile_rows] + jnp.pad(rim.astype(F32), ((0, 0), (0, tile_rows - win), (0, 0)))
    return (object_grad, probe_grad)


def solution(mesh):
    placed = (
        P(None, "rows", "cols"),
        P(),
        P("rows", "cols", None, None),
        P("rows", "cols"),
        P("rows", "cols"),
        P("rows", "cols"),
    )
    return jax.shard_map(
        local, mesh=mesh, in_specs=placed, out_specs=(P(None, "rows", "cols"), P()), check_vma=False
    )
```

```python
import functools

import jax
import jax.numpy as jnp
import ml_dtypes
import numpy as np
from jax import lax
from jax.experimental import pallas as pl
from jax.experimental.pallas import tpu as pltpu
from jax.sharding import PartitionSpec as P

F32 = jnp.float32
BF16 = jnp.bfloat16
LANES = 128
CHUNK = 16
BLOCK = 64


def dft_tables(win):
    half = win // 2
    k = np.arange(win)[:, None]
    j = np.arange(win)[None, :]
    angle = (k * j % win).astype(np.float64) * (2.0 * np.pi / win)
    re = np.cos(angle) / np.sqrt(win)
    im = -np.sin(angle) / np.sqrt(win)
    tables = []
    for parity in range(2):
        cr = re[parity::2, :half]
        ci = im[parity::2, :half]
        tables.append(np.block([[cr, -ci], [ci, cr]]))
    forward = np.stack(tables)
    backward = np.stack([t.T for t in tables])
    order = np.concatenate([np.arange(0, win, 2), np.arange(1, win, 2)])
    permute = np.zeros((win, win))
    permute[np.arange(win), order] = 1.0
    both = np.stack([permute, permute.T])
    cast = lambda a: a.astype(ml_dtypes.bfloat16)
    return cast(forward), cast(backward), cast(both)


def slots_kernel(
    info, fwd, bwd, probe, meas, own, own_low, nxt, nxt_low, sec, sec_low,
    g_own, g_next, g_next_low, g_sec, acc_keep, acc_send,
    ext, mid, acc, owin, xs, hb, gb, kb,
):
    slots = meas.shape[0]
    live = info[2 * slots]
    core = info[2 * slots + 1]
    modes = probe.shape[1]
    win = probe.shape[2]
    half = win // 2
    blocks = win // BLOCK
    tile_rows = own.shape[1]
    sums = (g_own, mid, g_sec)

    for c in range(2):
        for t, (top, bottom) in enumerate(((own, own_low), (nxt, nxt_low), (sec, sec_low))):
            ext[c, t, :tile_rows, :] = top[c].astype(F32)
            ext[c, t, tile_rows:, :] = bottom[c].astype(F32)
    for ref in sums + (acc,):
        ref[...] = jnp.zeros_like(ref)

    sides = (slice(0, LANES), slice(LANES, 2 * LANES))
    lane = lax.broadcasted_iota(jnp.int32, (CHUNK, LANES), 1)

    def pair_of_slots(pair, _):
        whole = 2 * pair + 1 < live
        slot = (2 * pair, jnp.where(whole, 2 * pair + 1, 2 * pair))
        weight = (None, jnp.where(whole, 1.0, 0.0).astype(F32))
        row = [info[s] for s in slot]
        col = [info[slots + s] for s in slot]
        left_shift = [lax.rem(LANES - c, LANES) for c in col]
        keep_left = [lane < LANES - c for c in col]
        keep_right = [lane >= c for c in col]

        for q in range(2):
            for at in range(0, win, CHUNK):
                for c in range(2):
                    parts = [
                        pltpu.roll(ext[c, t, pl.ds(row[q] + at, CHUNK), :], left_shift[q], 1) for t in range(3)
                    ]
                    for h in range(2):
                        owin[q, c, h, at : at + CHUNK, :] = jnp.where(keep_left[q], parts[h], parts[h + 1])

        for m in range(modes):
            for at in range(0, half, CHUNK):
                for h in range(2):
                    psi = ([], [])
                    for rows in (slice(at, at + CHUNK), slice(half + at, half + at + CHUNK)):
                        p_re = probe[0, m, rows, sides[h]]
                        p_im = probe[1, m, rows, sides[h]]
                        for q in range(2):
                            o_re = owin[q, 0, h, rows, :]
                            o_im = owin[q, 1, h, rows, :]
                            psi[q].append((p_re * o_re - p_im * o_im, p_re * o_im + p_im * o_re))
                    for q in range(2):
                        for c in range(2):
                            rows = slice(c * half + at, c * half + at + CHUNK)
                            xs[q, m, 0, rows, sides[h]] = (psi[q][0][c] + psi[q][1][c]).astype(BF16)
                            xs[q, m, 1, rows, sides[h]] = (psi[q][0][c] - psi[q][1][c]).astype(BF16)
            for q in range(2):
                for rp in range(2):
                    v = jnp.dot(fwd[rp], xs[q, m, rp], preferred_element_type=F32)
                    v = (
                        (v[:, :half] + v[:, half:]).astype(BF16),
                        (v[:, :half] - v[:, half:]).astype(BF16),
                    )
                    for pc in range(2):
                        for at in range(0, half, BLOCK):
                            for c in range(2):
                                hb[
                                    q, pc, (rp * half + at) // BLOCK, m * BLOCK : (m + 1) * BLOCK, sides[c]
                                ] = v[pc][c * half + at : c * half + at + BLOCK]

        for rb in range(blocks):
            for pc in range(2):
                for q in range(2):
                    field = jnp.dot(hb[q, pc, rb], bwd[pc], preferred_element_type=F32)
                    for at in range(0, BLOCK, CHUNK):
                        part = [field[m * BLOCK + at : m * BLOCK + at + CHUNK] for m in range(modes)]
                        total = 1.0
                        for f in part:
                            total = total + (f[:, :half] * f[:, :half] + f[:, half:] * f[:, half:])
                        f_row = rb * BLOCK + at
                        factor = 1.0 - meas[slot[q], f_row : f_row + CHUNK, sides[pc]].astype(F32) * lax.rsqrt(total)
                        if q == 1:
                            factor = factor * weight[q]
                        rp, f_row = divmod(f_row, half)
                        for m in range(modes):
                            for c in range(2):
                                gb[q, m, rp, c * half + f_row : c * half + f_row + CHUNK, sides[pc]] = (
                                    part[m][:, sides[c]] * factor
                                ).astype(BF16)

        for m in range(modes):
            for q in range(2):
                v0 = jnp.dot(bwd[0], gb[q, m, 0], preferred_element_type=F32)
                v1 = jnp.dot(bwd[1], gb[q, m, 1], preferred_element_type=F32)
                for side, v in enumerate(((v0 + v1).astype(BF16), (v0 - v1).astype(BF16))):
                    for at in range(0, half, BLOCK):
                        for pc in range(2):
                            for c in range(2):
                                kb[
                                    q, pc, (side * half + at) // BLOCK, m * BLOCK : (m + 1) * BLOCK, sides[c]
                                ] = v[c * half + at : c * half + at + BLOCK, sides[pc]]

        for rb in range(blocks):
            w = [
                [jnp.dot(kb[q, pc, rb], fwd[pc], preferred_element_type=F32) for pc in range(2)]
                for q in range(2)
            ]
            for at in range(0, BLOCK, CHUNK):
                rows = slice(rb * BLOCK + at, rb * BLOCK + at + CHUNK)
                g = [[[None, None], [None, None]] for q in range(2)]
                for h in range(2):
                    o = [[owin[q, c, h, rows, :] for c in range(2)] for q in range(2)]
                    for m in range(modes):
                        p_re = probe[0, m, rows, sides[h]]
                        p_im = probe[1, m, rows, sides[h]]
                        terms = []
                        for q in range(2):
                            w0, w1 = (v[m * BLOCK + at : m * BLOCK + at + CHUNK] for v in w[q])
                            chi = w0 + w1 if h == 0 else w0 - w1
                            c_re = chi[:, :half]
                            c_im = chi[:, half:]
                            t_re = p_re * c_re + p_im * c_im
                            t_im = p_re * c_im - p_im * c_re
                            g[q][0][h] = t_re if m == 0 else g[q][0][h] + t_re
                            g[q][1][h] = t_im if m == 0 else g[q][1][h] + t_im
                            o_re, o_im = o[q]
                            terms.append((o_re * c_re + o_im * c_im, o_re * c_im - o_im * c_re))
                        for c in range(2):
                            acc[c, m, rows, sides[h]] += terms[0][c] + terms[1][c]
                for q in range(2):
                    for c in range(2):
                        left = pltpu.roll(g[q][c][0], col[q], 1)
                        right = pltpu.roll(g[q][c][1], col[q], 1)
                        zero = jnp.zeros_like(left)
                        spread = (
                            jnp.where(keep_right[q], left, zero),
                            jnp.where(keep_right[q], right, left),
                            jnp.where(keep_right[q], zero, right),
                        )
                        for t in range(3):
                            sums[t][c, pl.ds(row[q] + rows.start, CHUNK), :] += spread[t]
        return 0

    lax.fori_loop(0, lax.div(live + 1, 2), pair_of_slots, 0)

    g_next[...] = mid[:, :tile_rows, :].astype(BF16)
    g_next_low[...] = mid[:, tile_rows:, :].astype(BF16)
    for m in range(modes):
        for at in range(0, win, 8):
            for h in range(2):
                to = (m * win + at) * 2 + 8 * h
                acc_keep[to : to + 8, :] = acc[core, m, at : at + 8, h * LANES : (h + 1) * LANES]
            pair = acc[1 - core, m, at : at + 8, :]
            to = (m * win + at) * 2
            acc_send[to : to + 16, :] = jnp.concatenate([pair[:, :LANES], pair[:, LANES:]], axis=0).astype(BF16)


def prepare_kernel(fwd, bwd, perm, probe, meas, fwd_out, bwd_out, probe_out, meas_out, swaps, raw, sems):
    copies = [
        pltpu.make_async_copy(source, target, sems.at[i])
        for i, (source, target) in enumerate(
            ((perm, swaps), (meas.at[0], raw), (probe, probe_out), (fwd, fwd_out), (bwd, bwd_out))
        )
    ]
    for copy in copies:
        copy.start()
    copies[0].wait()
    copies[1].wait()
    for s in range(raw.shape[0]):
        rows_done = jnp.dot(swaps[0], raw[s], preferred_element_type=F32).astype(BF16)
        meas_out[s] = jnp.dot(rows_done, swaps[1], preferred_element_type=F32).astype(BF16)
    for copy in copies[2:]:
        copy.wait()


def prepare(probe, measured):
    slots, win = measured.shape[1:3]
    fwd, bwd, perm = dft_tables(win)
    return pl.pallas_call(
        prepare_kernel,
        in_specs=[pl.BlockSpec(memory_space=pltpu.HBM)] * 5,
        out_specs=[pl.BlockSpec(memory_space=pltpu.VMEM)] * 4,
        out_shape=[
            jax.ShapeDtypeStruct(fwd.shape, BF16),
            jax.ShapeDtypeStruct(bwd.shape, BF16),
            jax.ShapeDtypeStruct(probe.shape, F32),
            jax.ShapeDtypeStruct(measured.shape[1:], BF16),
        ],
        scratch_shapes=[
            pltpu.VMEM(perm.shape, BF16),
            pltpu.VMEM(measured.shape[1:], BF16),
            pltpu.SemaphoreType.DMA((5,)),
        ],
        cost_estimate=pl.CostEstimate(flops=4 * slots * win**3, bytes_accessed=8 << 20, transcendentals=0),
        compiler_params=pltpu.CompilerParams(vmem_limit_bytes=8 * 1024 * 1024),
        name="prepare",
    )(jnp.asarray(fwd), jnp.asarray(bwd), jnp.asarray(perm), probe, measured)


def run_slots(info, fwd, bwd, probe, measured, own, own_low, nxt, nxt_low, sec, sec_low):
    tile_rows, tile_cols = own.shape[1:]
    modes, win = probe.shape[1:3]
    tall = (2, tile_rows + win, tile_cols)
    flat = (2 * modes * win, LANES)
    blocks = (2, win // BLOCK, modes * BLOCK, win)
    vmem = pl.BlockSpec(memory_space=pltpu.VMEM)
    return pl.pallas_call(
        slots_kernel,
        in_specs=[pl.BlockSpec(memory_space=pltpu.SMEM)] + [vmem] * 10,
        out_specs=[vmem] * 6,
        out_shape=[
            jax.ShapeDtypeStruct(tall, F32),
            jax.ShapeDtypeStruct(own.shape, BF16),
            jax.ShapeDtypeStruct(own_low.shape, BF16),
            jax.ShapeDtypeStruct(tall, F32),
            jax.ShapeDtypeStruct(flat, F32),
            jax.ShapeDtypeStruct(flat, BF16),
        ],
        scratch_shapes=[
            pltpu.VMEM((2, 3) + tall[1:], F32),
            pltpu.VMEM(tall, F32),
            pltpu.VMEM((2, modes, win, win), F32),
            pltpu.VMEM((2, 2, 2, win, LANES), F32),
            pltpu.VMEM((2, modes, 2, win, win), BF16),
            pltpu.VMEM((2,) + blocks, BF16),
            pltpu.VMEM((2, modes, 2, win, win), BF16),
            pltpu.VMEM((2,) + blocks, BF16),
        ],
        compiler_params=pltpu.CompilerParams(vmem_limit_bytes=22 * 1024 * 1024),
        name="slots",
    )(info, fwd, bwd, probe, measured, own, own_low, nxt, nxt_low, sec, sec_low)


def moved(value, target):
    n_rows = lax.axis_size("rows")
    n_cols = lax.axis_size("cols")
    pairs = []
    for a in range(n_rows):
        for b in range(n_cols):
            to_a, to_b = target(a, b)
            if 0 <= to_a < n_rows and 0 <= to_b < n_cols:
                pairs.append((a * n_cols + b, to_a * n_cols + to_b))
    return lax.ppermute(value, ("rows", "cols"), pairs)


def swap_cores(value):
    return moved(value, lambda a, b: (a, b ^ 1))


def local(object_field, probe_mode_stack, measured, corner_row, corner_col, count):
    tile_rows, tile_cols = object_field.shape[1:]
    modes, win = probe_mode_stack.shape[1:3]
    slot_count = measured.shape[1]
    devices = lax.axis_size("rows") * lax.axis_size("cols")
    col_at = lax.axis_index("cols")
    core = lax.rem(col_at, 2)

    top = object_field[:, :win, :]
    sec = moved(object_field, lambda a, b: (a, b - 2))
    sec_low = moved(top, lambda a, b: (a - 1, b - 2))
    own_low = moved(top, lambda a, b: (a - 1, b))
    prepared, sec = lax.optimization_barrier((prepare(probe_mode_stack, measured), sec))
    nxt_low = swap_cores(jnp.where(core == 0, sec_low, own_low))
    nxt = swap_cores(jnp.where(core == 0, sec, object_field))
    info = jnp.concatenate(
        [
            corner_row[0] - lax.axis_index("rows") * tile_rows,
            corner_col[0] - col_at * tile_cols,
            count[0],
            core[None],
        ]
    )
    g_own, g_next, g_next_low, g_sec, acc_keep, acc_send = run_slots(
        info, *prepared, object_field, own_low, nxt, nxt_low, sec, sec_low
    )

    acc_got = swap_cores(acc_send)
    near = swap_cores(g_next)
    chip_sum = (acc_keep + acc_got.astype(F32)).astype(BF16)
    chip_sum, near, near_low = lax.optimization_barrier((chip_sum, near, g_next_low))
    near = lax.optimization_barrier(jnp.concatenate([near, swap_cores(near_low)], axis=1).astype(F32))
    none = jnp.zeros_like(near)
    outward = (g_sec + jnp.where(core == 0, near, none)).astype(BF16)
    far = moved(outward, lambda a, b: (a, b + 2))
    total = g_own + jnp.where(core == 1, near, none) + far.astype(F32)
    rim = moved(total[:, tile_rows:].astype(BF16), lambda a, b: (a + 1, b))

    groups = [[i for i in range(devices) if i % 2 == c] for c in range(2)]
    exchange = functools.partial(
        lax.all_to_all, axis_name=("rows", "cols"), split_axis=0, concat_axis=0,
        axis_index_groups=groups, tiled=True,
    )
    share = exchange(chip_sum.reshape(devices // 2, -1, LANES))
    scale = 1.0 / jnp.sqrt(jnp.float32(devices * slot_count))
    share = (jnp.sum(share.astype(F32), axis=0) * scale).astype(BF16)
    mine = exchange(jnp.broadcast_to(share[None], (devices // 2,) + share.shape))
    mine, rim = lax.optimization_barrier((mine, rim))
    mine = mine.reshape(-1, LANES)
    part = lax.broadcasted_iota(jnp.int32, (2,) + mine.shape, 0)
    probe_grad = jnp.where(part == core, mine[None], swap_cores(mine)[None]).astype(F32)
    probe_grad = probe_grad.reshape(2, modes, win // 8, 2, 8, LANES).transpose(0, 1, 2, 4, 3, 5)
    probe_grad = probe_grad.reshape(2, modes, win, win)

    object_grad = total[:, :tile_rows] + jnp.pad(rim.astype(F32), ((0, 0), (0, tile_rows - win), (0, 0)))
    return (object_grad, probe_grad)


def solution(mesh):
    placed = (
        P(None, "rows", "cols"),
        P(),
        P("rows", "cols", None, None),
        P("rows", "cols"),
        P("rows", "cols"),
        P("rows", "cols"),
    )
    return jax.shard_map(
        local, mesh=mesh, in_specs=placed, out_specs=(P(None, "rows", "cols"), P()), check_vma=False
    )
```
